32 devices in a mesh: rep: 2 (over y), dp: 4 (over z), tp: 4 (over x, core).
Axes of the slice: x: 2, y: 2, z: 4, core: 2. Of those that a mesh axis runs over, the one named last changes fastest.
Arguments:
- hidden: bfloat16 [4, 512, 8192], P(None, ('rep', 'dp'), 'tp'), parts along dimension 1, may hold values from -6 to 6
- queries: bfloat16 [4, 512, 8192], P(None, ('rep', 'dp'), 'tp'), parts along dimension 1, may hold values from -8 to 8
- projection: bfloat16 [8192, 2048], P('tp'), may hold values from -0.0625 to 0.0625
- cached_key_rows: bfloat16 [512, 8, 128, 128], P(('rep', 'dp'), 'tp'), parts along dimension 0, may hold values from -8 to 8
- cached_value_rows: bfloat16 [512, 8, 128, 128], P(('rep', 'dp'), 'tp'), parts along dimension 0, may hold values from -6 to 6
- adapter_shrink_weight: bfloat16 [128, 16, 8192], P('dp', None, 'tp'), may hold values from -0.0625 to 0.0625
- adapter_expand_weight: bfloat16 [128, 16, 2048], P('dp', None, 'tp'), may hold values from -1.5 to 1.5
- requests: int32 [512], P(('rep', 'dp')), parts along dimension 0, may hold values from 0 to 127, as said below
- adapter_store_row: int32 [256], P('rep'), parts along dimension 0, may hold values from 0 to 127, as said below
- lengths: int32 [512], P(('rep', 'dp')), parts along dimension 0, may hold values from 2 to 128, as said below
Outputs:
- attended: bfloat16 [4, 512, 8192], P(None, ('rep', 'dp'), 'tp'), parts along dimension 1
- new_key_value: bfloat16 [4, 512, 2048], P(None, ('rep', 'dp'), 'tp'), parts along dimension 1
The draws below stay inside these ranges and needn't reach their ends.
There are 2 independent parts, one for each index of `rep`. The reference program is written for one: setup_inputs(seed, part) draws one part's arguments, and reference() takes and returns one part's arrays. A program takes and returns all parts, laid end to end along the dimension named above; an argument that names none is the same for every part. Nothing has to cross between parts.
Inputs may be any that keep to these rules, and one draw needn't show every extreme that they name: `requests`: in the block of 64 sequences of each dp index, at most 16 sequences use adapters whose store rows lie in any one dp index's block of 32 rows, and in every draw one such block serves exactly 16 sequences of every dp index. `adapter_store_row`: A permutation: every store row holds exactly one adapter. `lengths`: some sequence uses all 128 positions in every draw.
All inputs are finite; a program needn't handle non-finite values.
Results may differ from the reference program's by a relative error of at most 0.006.
Values may be sent and summed in bfloat16 or wider, within the bound.
No kernel may reach another device: no remote copies, remote signals or barrier semaphores. Data moves between devices by JAX's collectives and lax.ppermute only.
A program may use at most 128 MiB of HBM per device.

```python
import math
import jax
import jax.numpy as jnp
from jax import lax

MODEL_WIDTH = 8192
HEADS = 64
KVH = 8
HD = 128
ADAPTER_RANK = 16
ADP = 32
STEPS = 4
SEQ_DEV = 64
CACHE = 128
SEQS = 256
ADAPTER_TOTAL = 128
KEY_VALUE_WIDTH = 2048
CAP = 16
N_DP = 4


def adapter_order(key):
    return jax.random.permutation(jax.random.fold_in(key, 201), ADAPTER_TOTAL).astype(jnp.int32)


def draw_queries(key, part):
    key = jax.random.fold_in(key, 1)
    values = jax.random.normal(key, (STEPS, SEQS, HEADS * HD))
    return jnp.clip(values, -8.0, 8.0).astype(jnp.bfloat16)


def draw_cached_key_rows(key, part):
    key = jax.random.fold_in(key, 2)
    values = jax.random.normal(key, (SEQS, KVH, CACHE, HD))
    return jnp.clip(values, -8.0, 8.0).astype(jnp.bfloat16)


def draw_adapter_store_row(key, part):
    order = adapter_order(key)
    return order


def draw_requests(key, part):
    order = adapter_order(key)
    key = jax.random.fold_in(key, 5)
    inverse = jnp.argsort(order).astype(jnp.int32)
    hottest = jax.random.randint(jax.random.fold_in(key, 1), (), 0, N_DP)
    others = (hottest + 1 + jnp.arange(N_DP - 1, dtype=jnp.int32)) % N_DP
    reserve = jnp.repeat(others, CAP)

    def choose_owners(subkey):
        return jax.random.permutation(subkey, reserve)[:SEQ_DEV - CAP]
    picks = jax.vmap(choose_owners)(jax.random.split(jax.random.fold_in(key, 2), N_DP))
    owners = jnp.concatenate([jnp.full((N_DP, CAP), hottest, dtype=jnp.int32), picks.astype(jnp.int32)], axis=1)

    def shuffle_owners(subkey, listed):
        return jax.random.permutation(subkey, listed)
    owners = jax.vmap(shuffle_owners)(jax.random.split(jax.random.fold_in(key, 3), N_DP), owners)
    slots = jax.random.randint(jax.random.fold_in(key, 4), (N_DP, SEQ_DEV), 0, ADP)
    return inverse[(owners * ADP + slots).reshape(SEQS)].astype(jnp.int32)


def draw_lengths(key, part):
    key = jax.random.fold_in(key, 7)
    drawn = jax.random.randint(jax.random.fold_in(key, 1), (SEQS,), 2, CACHE + 1)
    fullest = jax.random.randint(jax.random.fold_in(key, 2), (), 0, SEQS)
    return drawn.at[fullest].set(CACHE).astype(jnp.int32)


def block_scale(rng, extent, cuts, smallest, top_value):
    def one(dim, parts):
        draws = jax.random.uniform(jax.random.fold_in(jax.random.fold_in(rng, 6), dim), (parts,), jnp.float32, smallest / len(cuts), top_value / len(cuts))
        return jnp.repeat(jnp.exp(draws), extent[dim] // parts).reshape((-1,) + (1,) * (len(extent) - dim - 1))

    loudness = one(*cuts[0])
    for cut in cuts[1:]:
        loudness = loudness * one(*cut)
    return loudness


def normal_values(rng, shape, scale, bound, shards=(), kind=jnp.bfloat16):
    values = jax.random.normal(rng, shape, jnp.float32) * scale
    if len(shards) > 0:
        values = block_scale(rng, shape, shards, -0.22, 0.18) * values
    return jnp.clip(values, min=-bound, max=bound).astype(kind)


def setup_inputs(seed: int = 0, part: int = 0) -> dict:
    streams_of = jax.random.split(jax.random.key(seed), 11)
    part_keys = jax.random.split(jax.random.fold_in(streams_of[10], part), 11)
    return {
        "hidden": normal_values(part_keys[0], (STEPS, SEQS, MODEL_WIDTH), 1.0, 6.0, ((1, 4), (2, 4))),
        "queries": draw_queries(jax.random.fold_in(jax.random.fold_in(streams_of[10], part), 71), part),
        "projection": normal_values(streams_of[2], (MODEL_WIDTH, KEY_VALUE_WIDTH), MODEL_WIDTH ** -0.5, 0.0625, ((0, 4),)),
        "cached_key_rows": draw_cached_key_rows(jax.random.fold_in(jax.random.fold_in(streams_of[10], part), 71), part),
        "cached_value_rows": normal_values(part_keys[4], (SEQS, KVH, CACHE, HD), 1.0, 6.0, ((0, 4), (1, 4))),
        "adapter_shrink_weight": normal_values(streams_of[5], (ADAPTER_TOTAL, ADAPTER_RANK, MODEL_WIDTH), MODEL_WIDTH ** -0.5, 0.0625, ((0, 4), (2, 4))),
        "adapter_expand_weight": normal_values(streams_of[6], (ADAPTER_TOTAL, ADAPTER_RANK, KEY_VALUE_WIDTH), ADAPTER_RANK ** -0.5, 1.5, ((0, 4), (2, 4))),
        "requests": draw_requests(jax.random.fold_in(jax.random.fold_in(streams_of[10], part), 71), part),
        "adapter_store_row": draw_adapter_store_row(jax.random.fold_in(jax.random.fold_in(streams_of[10], part), 71), part),
        "lengths": draw_lengths(jax.random.fold_in(jax.random.fold_in(streams_of[10], part), 71), part),
    }


adapter_scale = 0.5

def attend(query_heads, cached_key_rows, cached_value_rows, fresh_keys, fresh_values, lengths):
    step_count = query_heads.shape[0]
    scaling = 1.0 / math.sqrt(query_heads.shape[-1])
    heads_float = query_heads.astype(jnp.float32)
    past = jnp.einsum('sbhgd,bhpd->sbhgp', heads_float, cached_key_rows.astype(jnp.float32)) * scaling
    fresh = jnp.einsum('sbhgd,tbhd->sbhgt', heads_float, fresh_keys.astype(jnp.float32)) * scaling
    live = jnp.arange(cached_key_rows.shape[2], dtype=jnp.int32)[None, :] < lengths[:, None]
    past = jnp.where(live[None, :, None, None, :], past, -jnp.inf)
    causal = jnp.arange(step_count)[None, :] <= jnp.arange(step_count)[:, None]
    fresh = jnp.where(causal[:, None, None, None, :], fresh, -jnp.inf)
    highest = jnp.maximum(lax.optimization_barrier(jnp.max(past, axis=-1)), lax.optimization_barrier(jnp.max(fresh, axis=-1)))[..., None]
    past_exp = jnp.exp(past - highest)
    fresh_exp = jnp.exp(fresh - highest)
    total = lax.optimization_barrier(jnp.sum(past_exp, axis=-1, keepdims=True)) + lax.optimization_barrier(jnp.sum(fresh_exp, axis=-1, keepdims=True))
    past_weights = (past_exp / total).astype(jnp.bfloat16).astype(jnp.float32)
    fresh_weights = (fresh_exp / total).astype(jnp.bfloat16).astype(jnp.float32)
    mixed = jnp.einsum('sbhgp,bhpd->sbhgd', past_weights, cached_value_rows.astype(jnp.float32))
    mixed = mixed + jnp.einsum('sbhgt,tbhd->sbhgd', fresh_weights, fresh_values.astype(jnp.float32))
    return mixed.astype(jnp.bfloat16)

def reference(hidden, queries, projection, cached_key_rows, cached_value_rows, adapter_shrink_weight, adapter_expand_weight, requests, adapter_store_row, lengths):
    matches = requests[:, None] == jnp.arange(ADAPTER_TOTAL, dtype=jnp.int32)[None, :]
    store_rows = lax.optimization_barrier(jnp.sum(jnp.where(matches, adapter_store_row[None, :], 0), axis=1)).astype(jnp.int32)
    base = jnp.dot(hidden.reshape(STEPS * SEQS, MODEL_WIDTH), projection, preferred_element_type=jnp.float32)
    base = base.reshape(STEPS, SEQS, KEY_VALUE_WIDTH)
    blocks = SEQS // SEQ_DEV

    def split(tensor, dimension):
        shaped = tensor.reshape(tensor.shape[:dimension] + (blocks, SEQ_DEV) + tensor.shape[dimension + 1:])
        return jnp.moveaxis(shaped, dimension, 0)

    def one_block(pieces):
        block_hidden, block_queries, block_base, block_keys, block_values, row_block_list, block_lengths = pieces
        shrink_factor_rows = adapter_shrink_weight[row_block_list].astype(jnp.float32)
        shrunken_input = jnp.einsum('snd,nrd->snr', block_hidden.astype(jnp.float32), shrink_factor_rows).astype(jnp.bfloat16)
        expand_factor_rows = adapter_expand_weight[row_block_list].astype(jnp.float32)
        adapter_update = (adapter_scale * jnp.einsum('ymo,mow->ymw', shrunken_input.astype(jnp.float32), expand_factor_rows)).astype(jnp.bfloat16)
        key_value = (block_base + adapter_update.astype(jnp.float32)).astype(jnp.bfloat16)
        paired = key_value.reshape(STEPS, SEQ_DEV, KVH, 2, HD)
        query_heads = block_queries.reshape(STEPS, SEQ_DEV, KVH, HEADS // KVH, HD)
        mixed = attend(query_heads, block_keys, block_values, paired[:, :, :, 0], paired[:, :, :, 1], block_lengths)
        return (mixed.reshape(STEPS, SEQ_DEV, HEADS * HD), key_value)
    mixed, key_value = lax.map(one_block, (split(hidden, 1), split(queries, 1), split(base, 1), split(cached_key_rows, 0), split(cached_value_rows, 0), split(store_rows, 0), split(lengths, 0)))
    attended = jnp.moveaxis(mixed, 0, 1).reshape(STEPS, SEQS, HEADS * HD)
    new_key_value = jnp.moveaxis(key_value, 0, 1).reshape(STEPS, SEQS, KEY_VALUE_WIDTH)
    return (attended, new_key_value)
```

```python
import functools
import math

import jax
import jax.numpy as jnp
from jax import lax
from jax.experimental import pallas as pl
from jax.experimental.pallas import tpu as pltpu
from jax.sharding import PartitionSpec as P

adapter_scale = 0.5
F32 = jnp.float32
BF16 = jnp.bfloat16
NT = (((1,), (1,)), ((), ()))
TN = (((0,), (0,)), ((), ()))
MIB = 1024 * 1024


def params(mib=40, **kw):
    return pltpu.CompilerParams(vmem_limit_bytes=mib * MIB, **kw)


def cost(flops, nbytes, transcendentals=0):
    return pl.CostEstimate(
        flops=int(flops), bytes_accessed=int(nbytes), transcendentals=int(transcendentals)
    )


def swap(axis, size, distance):
    pairs = [(i, i ^ distance) for i in range(size)]
    return lambda value: lax.ppermute(value, axis, pairs)


def iota(shape, dim):
    return lax.broadcasted_iota(jnp.int32, shape, dim)


def column(row):
    size = row.shape[1]
    diagonal = iota((size, size), 0) == iota((size, size), 1)
    return jnp.sum(jnp.where(diagonal, row, 0.0), axis=1, keepdims=True)


def route_kernel(groups, cap, entries, requests_ref, store_ref, hidden_ref, *outs):
    blocks, slots, back_ref = outs[:groups], outs[groups : 2 * groups], outs[2 * groups]
    steps, seqs, _ = hidden_ref.shape
    me = lax.axis_index("dp")
    store_col = column(store_ref[...].astype(F32))
    adapters = store_col.shape[0]
    rows = jnp.sum(
        jnp.where(iota((adapters, seqs), 0) == requests_ref[...], store_col, 0.0),
        axis=0,
        keepdims=True,
    ).astype(jnp.int32)
    owner = lax.div(rows, jnp.int32(entries))
    slot_col = column((rows - owner * entries).astype(F32))
    distance = jnp.bitwise_xor(owner, me).astype(F32)
    distance_col = column(distance)
    before = (distance_col == distance) & (iota((seqs, seqs), 0) < iota((seqs, seqs), 1))
    rank = jnp.sum(jnp.where(before, 1.0, 0.0), axis=0, keepdims=True)
    bucket = distance * cap + rank
    bucket_col = column(bucket).astype(jnp.int32)
    bucket = bucket.astype(jnp.int32)
    placed = jnp.where(iota((groups * cap, seqs), 0) == bucket, 1.0, 0.0).astype(BF16)
    back_ref[...] = jnp.where(bucket_col == iota((seqs, groups * cap), 1), 1.0, 0.0).astype(BF16)
    for k in range(groups):
        spot = lax.rem(iota((seqs, steps * cap), 1), jnp.int32(cap)) + k * cap
        slots[k][...] = jnp.sum(
            jnp.where(bucket_col == spot, slot_col, 0.0), axis=0, keepdims=True
        ).astype(jnp.int32)
    for s in range(steps):
        picked = jnp.dot(placed, hidden_ref[s], preferred_element_type=F32).astype(BF16)
        for k in range(groups):
            blocks[k][s * cap : (s + 1) * cap, :] = picked[k * cap : (k + 1) * cap, :]


def route(requests, store, hidden, groups, cap, entries):
    steps, seqs, features = hidden.shape
    rows = steps * cap
    return pl.pallas_call(
        functools.partial(route_kernel, groups, cap, entries),
        out_shape=[jax.ShapeDtypeStruct((rows, features), BF16)] * groups
        + [jax.ShapeDtypeStruct((1, rows), jnp.int32)] * groups
        + [jax.ShapeDtypeStruct((seqs, groups * cap), BF16)],
        compiler_params=params(),
        cost_estimate=cost(
            2 * groups * cap * seqs * steps * features, 4 * steps * seqs * features
        ),
        name="route",
    )(requests[None, :], store[None, :], hidden)


def base_kernel(tp_ref, hidden_ref, projection_ref, out_ref):
    out_ref[0] = jnp.dot(hidden_ref[...], projection_ref[...], preferred_element_type=F32)


def base_part(tp_index, hidden, projection, size, low):
    rows, features = hidden.shape
    width = projection.shape[1] // size
    count = size // 2
    cuts = 2
    piece = width // cuts

    def pick(i, j, tp):
        return (0, jnp.bitwise_xor(tp[0], 2 * i + low) * cuts + j)

    return pl.pallas_call(
        base_kernel,
        grid_spec=pltpu.PrefetchScalarGridSpec(
            num_scalar_prefetch=1,
            grid=(count, cuts),
            in_specs=[
                pl.BlockSpec((rows, features), lambda i, j, tp: (0, 0)),
                pl.BlockSpec((features, piece), pick),
            ],
            out_specs=pl.BlockSpec((1, rows, piece), lambda i, j, tp: (i, 0, j)),
        ),
        out_shape=jax.ShapeDtypeStruct((count, rows, width), F32),
        compiler_params=params(),
        cost_estimate=cost(
            2 * rows * features * width * count,
            2 * features * width * count + 2 * rows * features + 4 * rows * width * count,
        ),
        name="base_sent" if low else "base_kept",
    )(tp_index, hidden, projection)


def past_kernel(lengths_ref, query_ref, key_ref, value_ref, mixed_ref, lse_ref):
    steps, chunk, width = query_ref.shape
    _, heads, positions, size = key_ref.shape
    total_heads = width // size
    share = total_heads // heads
    first = pl.program_id(0) * chunk
    scaling = 1.0 / math.sqrt(size)
    by_seq = []
    for s in range(steps):
        whole = query_ref[s].astype(F32)
        stacked = jnp.stack(
            [whole[:, i * size : (i + 1) * size] for i in range(total_heads)], axis=0
        )
        by_seq.append(jnp.swapaxes(stacked, 0, 1))
    mixed_rows = [[] for _ in range(steps)]
    lse_rows = [[] for _ in range(steps)]
    for i in range(chunk):
        live = iota((steps * share, positions), 1) < lengths_ref[first + i]
        parts = []
        lses = []
        for g in range(heads):
            q = jnp.concatenate(
                [by_seq[s][i, g * share : (g + 1) * share, :] for s in range(steps)], axis=0
            ).astype(BF16)
            scores = (
                lax.dot_general(q, key_ref[i, g], NT, preferred_element_type=F32) * scaling
            )
            scores = jnp.where(live, scores, -jnp.inf)
            top = jnp.max(scores, axis=1, keepdims=True)
            raised = jnp.exp(scores - top)
            total = jnp.sum(raised, axis=1, keepdims=True)
            mixed = jnp.dot(
                raised.astype(BF16), value_ref[i, g], preferred_element_type=F32
            )
            parts.append(mixed / total)
            lses.append(jnp.broadcast_to(top + jnp.log(total), (steps * share, size)))
        for s in range(steps):
            cut = slice(s * share, (s + 1) * share)
            mixed_rows[s].append(jnp.concatenate([p[cut] for p in parts], axis=0))
            lse_rows[s].append(jnp.concatenate([p[cut] for p in lses], axis=0))
    lane = iota((chunk, size), 1)
    for s in range(steps):
        mixed = jnp.swapaxes(jnp.stack(mixed_rows[s], axis=0), 0, 1)
        lse = jnp.swapaxes(jnp.stack(lse_rows[s], axis=0), 0, 1)
        packed = jnp.zeros((chunk, size), F32)
        for i in range(total_heads):
            mixed_ref[s, :, i * size : (i + 1) * size] = mixed[i]
            packed = jnp.where(lane == i, lse[i], packed)
        lse_ref[s] = packed


def past(lengths, queries, keys, values):
    steps, seqs, width = queries.shape
    _, heads, positions, size = keys.shape
    chunk = 8
    cache_spec = pl.BlockSpec((chunk, heads, positions, size), lambda i, n: (i, 0, 0, 0))
    return pl.pallas_call(
        past_kernel,
        grid_spec=pltpu.PrefetchScalarGridSpec(
            num_scalar_prefetch=1,
            grid=(seqs // chunk,),
            in_specs=[
                pl.BlockSpec((steps, chunk, width), lambda i, n: (0, i, 0)),
                cache_spec,
                cache_spec,
            ],
            out_specs=[
                pl.BlockSpec((steps, chunk, width), lambda i, n: (0, i, 0)),
                pl.BlockSpec((steps, chunk, size), lambda i, n: (0, i, 0)),
            ],
        ),
        out_shape=[
            jax.ShapeDtypeStruct((steps, seqs, width), F32),
            jax.ShapeDtypeStruct((steps, seqs, size), F32),
        ],
        compiler_params=params(),
        cost_estimate=cost(
            4 * steps * seqs * width * positions,
            4 * seqs * heads * positions * size + 6 * steps * seqs * width,
            steps * seqs * (width // size) * positions,
        ),
        name="past",
    )(lengths, queries, keys, values)


def slot_mask(entries, rank, slots):
    return lax.div(iota((entries * rank, slots.shape[1]), 0), jnp.int32(rank)) == slots


def shrink_kernel(count, entries, rank, weight_ref, *refs):
    hidden, slots, out_ref = refs[:count], refs[count : 2 * count], refs[2 * count]
    rows = jnp.concatenate([r[...] for r in hidden], axis=0)
    slot = jnp.concatenate([r[...] for r in slots], axis=1)
    every = lax.dot_general(weight_ref[...], rows, NT, preferred_element_type=F32)
    kept = jnp.where(slot_mask(entries, rank, slot), every, 0.0)
    out_ref[...] = jnp.sum(kept.reshape(entries, rank, kept.shape[1]), axis=0)


def shrink(weight, hidden, slots):
    entries, rank, features = weight.shape
    count = len(hidden)
    rows = count * hidden[0].shape[0]
    return pl.pallas_call(
        functools.partial(shrink_kernel, count, entries, rank),
        out_shape=jax.ShapeDtypeStruct((rank, rows), F32),
        compiler_params=params(),
        cost_estimate=cost(
            2 * entries * rank * features * rows, 2 * features * (entries * rank + rows)
        ),
        name="shrink",
    )(weight.reshape(entries * rank, features), *hidden, *slots)


def expand_kernel(groups, size, entries, rank, weight_ref, *refs):
    parts, slots, outs = refs[:size], refs[size : size + groups], refs[size + groups :]
    total = parts[0][...]
    for part in parts[1:]:
        total = total + part[...]
    slot = jnp.concatenate([r[...] for r in slots], axis=1)
    shrunk = total.astype(BF16).astype(F32)
    spread = jnp.broadcast_to(shrunk[None], (entries,) + shrunk.shape).reshape(
        entries * rank, shrunk.shape[1]
    )
    spread = jnp.where(slot_mask(entries, rank, slot), spread, 0.0).astype(BF16)
    delta = adapter_scale * lax.dot_general(
        spread, weight_ref[...], TN, preferred_element_type=F32
    )
    delta = delta.astype(BF16)
    rows = outs[0].shape[0]
    for k in range(groups):
        outs[k][...] = delta[k * rows : (k + 1) * rows]


def expand(weight, parts, slots):
    entries, rank, columns = weight.shape
    groups = len(slots)
    rows = parts[0].shape[1] // groups
    return pl.pallas_call(
        functools.partial(expand_kernel, groups, len(parts), entries, rank),
        out_shape=[jax.ShapeDtypeStruct((rows, columns), BF16)] * groups,
        compiler_params=params(),
        cost_estimate=cost(
            2 * entries * rank * columns * rows * groups, 2 * entries * rank * columns
        ),
        name="expand",
    )(weight.reshape(entries * rank, columns), *parts, *slots)


def finish_kernel(
    groups, cap, heads, back_ref, own_ref, got_ref, query_ref, mixed_ref, lse_ref, *refs
):
    deltas, out_ref, new_ref = refs[:groups], refs[groups], refs[groups + 1]
    steps, seqs, width = query_ref.shape
    columns = new_ref.shape[2]
    size = columns // (2 * heads)
    share = width // (size * heads)
    scaling = 1.0 / math.sqrt(size)
    back = back_ref[...]
    new = []
    for s in range(steps):
        delta = jnp.concatenate([r[s * cap : (s + 1) * cap, :] for r in deltas], axis=0)
        update = jnp.dot(back, delta, preferred_element_type=F32)
        rows = slice(s * seqs, (s + 1) * seqs)
        base = own_ref[rows, :] + got_ref[rows, :].astype(F32)
        new.append((base + update).astype(BF16))
        new_ref[s] = new[s]
    for g in range(heads):
        left = g * 2 * size
        keys = jnp.concatenate([n[:, left : left + size] for n in new], axis=0)
        values = jnp.concatenate([n[:, left + size : left + 2 * size] for n in new], axis=0)
        for s in range(steps):
            fresh = (s + 1) * seqs
            same = lax.rem(iota((seqs, fresh), 1), jnp.int32(seqs)) == iota((seqs, fresh), 0)
            for h in range(share):
                head = g * share + h
                lanes = slice(head * size, (head + 1) * size)
                q = query_ref[s, :, lanes]
                scores = (
                    lax.dot_general(q, keys[:fresh], NT, preferred_element_type=F32) * scaling
                )
                scores = jnp.where(same, scores, -jnp.inf)
                lse = lse_ref[s, :, head : head + 1]
                top = jnp.maximum(jnp.max(scores, axis=1, keepdims=True), lse)
                raised = jnp.exp(scores - top)
                old = jnp.exp(lse - top)
                scale = 1.0 / (jnp.sum(raised, axis=1, keepdims=True) + old)
                weights = (raised * scale).astype(BF16)
                mixed = jnp.dot(weights, values[:fresh], preferred_element_type=F32)
                mixed = mixed + mixed_ref[s, :, lanes] * (old * scale)
                out_ref[s, :, lanes] = mixed.astype(BF16)


def finish(back, own, got, queries, mixed, lse, deltas, cap, heads):
    steps, seqs, width = queries.shape
    columns = own.shape[1]
    return pl.pallas_call(
        functools.partial(finish_kernel, len(deltas), cap, heads),
        out_shape=[
            jax.ShapeDtypeStruct((steps, seqs, width), BF16),
            jax.ShapeDtypeStruct((steps, seqs, columns), BF16),
        ],
        compiler_params=params(),
        cost_estimate=cost(
            4 * steps * seqs * width * steps * seqs,
            8 * steps * seqs * width + 8 * steps * seqs * columns,
            steps * seqs * width * 2,
        ),
        name="finish",
    )(back, own, got, queries, mixed, lse, *deltas)


def body(
    hidden,
    queries,
    projection,
    cached_key_rows,
    cached_value_rows,
    adapter_shrink_weight,
    adapter_expand_weight,
    requests,
    adapter_store_row,
    lengths,
):
    steps, seqs, features = hidden.shape
    groups = lax.axis_size("dp")
    size = lax.axis_size("tp")
    cap = seqs // 4
    entries = adapter_shrink_weight.shape[0]
    heads = cached_key_rows.shape[1]

    routed = route(requests, adapter_store_row, hidden, groups, cap, entries)
    blocks, slots, back = routed[:groups], routed[groups : 2 * groups], routed[2 * groups]
    over_dp = [None] + [swap("dp", groups, k) for k in range(1, groups)]
    over_tp = [None] + [swap("tp", size, k) for k in range(1, size)]
    order = sorted(range(1, groups), key=lambda k: -k)
    got_blocks = {0: blocks[0]}
    got_slots = {0: slots[0]}
    for k in order:
        got_blocks[k] = over_dp[k](blocks[k])
    for k in order:
        got_slots[k] = over_dp[k](slots[k])

    tp_index = lax.axis_index("tp").astype(jnp.int32).reshape(1)
    flat = hidden.reshape(steps * seqs, features)
    sent = base_part(tp_index, flat, projection, size, 1)
    kept = base_part(tp_index, flat, projection, size, 0)
    held = kept + over_tp[1](sent)
    distance = size // 2
    received = None
    while distance > 1:
        half = distance // 2
        received = over_tp[distance](held[half:].astype(BF16))
        if distance > 2:
            held = held[:half] + received.astype(F32)
        distance = half
    own, received = held[0], received[0]

    mixed, lse = past(lengths, queries, cached_key_rows, cached_value_rows)

    hidden_blocks = [got_blocks[k] for k in range(groups)]
    slot_blocks = [got_slots[k] for k in range(groups)]
    shrunk = shrink(adapter_shrink_weight, hidden_blocks, slot_blocks)
    parts = [shrunk] + [over_tp[k](shrunk) for k in range(1, size)]
    deltas = expand(adapter_expand_weight, parts, slot_blocks)
    deltas = [deltas[0]] + [over_dp[k](deltas[k]) for k in range(1, groups)]
    return tuple(finish(back, own, received, queries, mixed, lse, deltas, cap, heads))


def solution(mesh):
    placed = (
        P(None, ("rep", "dp"), "tp"),
        P(None, ("rep", "dp"), "tp"),
        P("tp", None),
        P(("rep", "dp"), "tp", None, None),
        P(("rep", "dp"), "tp", None, None),
        P("dp", None, "tp"),
        P("dp", None, "tp"),
        P(("rep", "dp")),
        P("rep"),
        P(("rep", "dp")),
    )
    return jax.shard_map(
        body,
        mesh=mesh,
        in_specs=placed,
        out_specs=(P(None, ("rep", "dp"), "tp"), P(None, ("rep", "dp"), "tp")),
        check_vma=False,
    )
```

```python
import functools
import math

import jax
import jax.numpy as jnp
from jax import lax
from jax.experimental import pallas as pl
from jax.experimental.pallas import tpu as pltpu
from jax.sharding import PartitionSpec as P

adapter_scale = 0.5
F32 = jnp.float32
BF16 = jnp.bfloat16
NT = (((1,), (1,)), ((), ()))
TN = (((0,), (0,)), ((), ()))
MIB = 1024 * 1024
LANES = 128


def params(mib):
    return pltpu.CompilerParams(vmem_limit_bytes=mib * MIB)


def cost(flops, nbytes, transcendentals=0):
    return pl.CostEstimate(
        flops=int(flops), bytes_accessed=int(nbytes), transcendentals=int(transcendentals)
    )


def swap(axis, size, distance):
    pairs = [(i, i ^ distance) for i in range(size)]
    return lambda value: lax.ppermute(value, axis, pairs)


def iota(shape, dim):
    return lax.broadcasted_iota(jnp.int32, shape, dim)


def column(row):
    size = row.shape[1]
    diagonal = iota((size, size), 0) == iota((size, size), 1)
    return jnp.sum(jnp.where(diagonal, row, 0.0), axis=1, keepdims=True)


def route_kernel(groups, cap, entries, requests_ref, store_ref, hidden_ref, *outs):
    blocks, back_ref = outs[:groups], outs[groups]
    steps, seqs, features = hidden_ref.shape
    tiles = features // LANES
    me = lax.axis_index("dp")
    store_col = column(store_ref[...].astype(F32))
    adapters = store_col.shape[0]
    rows = jnp.sum(
        jnp.where(iota((adapters, seqs), 0) == requests_ref[...], store_col, 0.0),
        axis=0,
        keepdims=True,
    ).astype(jnp.int32)
    owner = lax.div(rows, jnp.int32(entries))
    slot_col = column((rows - owner * entries).astype(F32))
    distance = jnp.bitwise_xor(owner, me).astype(F32)
    distance_col = column(distance)
    before = (distance_col == distance) & (iota((seqs, seqs), 0) < iota((seqs, seqs), 1))
    rank = jnp.sum(jnp.where(before, 1.0, 0.0), axis=0, keepdims=True)
    bucket = distance * cap + rank
    bucket_col = column(bucket).astype(jnp.int32)
    bucket = bucket.astype(jnp.int32)
    placed = jnp.where(iota((groups * cap, seqs), 0) == bucket, 1.0, 0.0).astype(BF16)
    back_ref[...] = jnp.where(bucket_col == iota((seqs, groups * cap), 1), 1.0, 0.0).astype(BF16)
    for k in range(groups):
        spot = lax.rem(iota((seqs, LANES), 1), jnp.int32(cap)) + k * cap
        slots = jnp.sum(jnp.where(bucket_col == spot, slot_col, 0.0), axis=0, keepdims=True)
        blocks[k][steps * tiles * cap :, :] = jnp.broadcast_to(slots, (cap, LANES)).astype(BF16)
    for s in range(steps):
        picked = jnp.dot(placed, hidden_ref[s], preferred_element_type=F32).astype(BF16)
        for k in range(groups):
            for c in range(tiles):
                first = (s * tiles + c) * cap
                blocks[k][first : first + cap, :] = picked[
                    k * cap : (k + 1) * cap, c * LANES : (c + 1) * LANES
                ]


def route(requests, store, hidden, groups, cap, entries):
    steps, seqs, features = hidden.shape
    rows = (steps * (features // LANES) + 1) * cap
    return pl.pallas_call(
        functools.partial(route_kernel, groups, cap, entries),
        out_shape=[jax.ShapeDtypeStruct((rows, LANES), BF16)] * groups
        + [jax.ShapeDtypeStruct((seqs, groups * cap), BF16)],
        compiler_params=params(10),
        cost_estimate=cost(
            2 * groups * cap * seqs * steps * features, 4 * steps * seqs * features
        ),
        name="route",
    )(requests[None, :], store[None, :], hidden)


def base_kernel(size, hidden_ref, projection_ref, *outs):
    width = outs[0].shape[1]
    me = lax.axis_index("tp")
    for k in list(range(1, size)) + [0]:
        first = pl.multiple_of(jnp.bitwise_xor(me, k) * width, width)
        part = jnp.dot(
            hidden_ref[...], projection_ref[:, pl.ds(first, width)], preferred_element_type=F32
        )
        outs[k][...] = part.astype(outs[k].dtype)


def base(hidden, projection, size):
    rows, _ = hidden.shape
    width = projection.shape[1] // size
    return pl.pallas_call(
        functools.partial(base_kernel, size),
        out_shape=[jax.ShapeDtypeStruct((rows, width), F32)]
        + [jax.ShapeDtypeStruct((rows, width), BF16)] * (size - 1),
        compiler_params=params(20),
        cost_estimate=cost(0, 4096),
        name="base",
    )(hidden, projection)


def past_kernel(lengths_ref, query_ref, key_ref, value_ref, mixed_ref, lse_ref):
    steps, chunk, width = query_ref.shape
    _, heads, positions, size = key_ref.shape
    share = width // (size * heads)
    rows = steps * share
    first = pl.program_id(0) * chunk
    scaling = 1.0 / math.sqrt(size)

    def lanes(g, h):
        return slice((g * share + h) * size, (g * share + h + 1) * size)

    by_seq = {}
    for s in range(steps):
        whole = query_ref[s].astype(F32)
        for g in range(heads):
            stacked = jnp.stack([whole[:, lanes(g, h)] for h in range(share)], axis=0)
            by_seq[s, g] = jnp.swapaxes(stacked, 0, 1)
    units = [(i, g) for i in range(chunk) for g in range(heads)]
    scores = []
    for i, g in units:
        q = jnp.concatenate([by_seq[s, g][i] for s in range(steps)], axis=0).astype(BF16)
        raw = lax.dot_general(q, key_ref[i, g], NT, preferred_element_type=F32) * scaling
        live = iota((rows, positions), 1) < lengths_ref[first + i]
        scores.append(jnp.where(live, raw, -jnp.inf))
    scores = jnp.concatenate(scores, axis=0)
    top = jnp.max(scores, axis=1, keepdims=True)
    raised = jnp.exp(scores - top)
    total = jnp.sum(raised, axis=1, keepdims=True)
    weights = raised.astype(BF16)
    mixed = [
        jnp.dot(weights[u * rows : (u + 1) * rows], value_ref[i, g], preferred_element_type=F32)
        for u, (i, g) in enumerate(units)
    ]
    mixed = jnp.concatenate(mixed, axis=0) * (1.0 / total)
    lse = jnp.broadcast_to(top + jnp.log(total), mixed.shape)
    mixed = mixed.reshape(chunk, heads, steps, share, size)
    lse = lse.reshape(chunk, heads, steps, share, size)
    for s in range(steps):
        for g in range(heads):
            mixed_by_head = jnp.swapaxes(mixed[:, g, s], 0, 1)
            lse_by_head = jnp.swapaxes(lse[:, g, s], 0, 1)
            for h in range(share):
                mixed_ref[s, :, lanes(g, h)] = mixed_by_head[h]
                lse_ref[s, :, lanes(g, h)] = lse_by_head[h]


def past(lengths, queries, keys, values):
    steps, seqs, width = queries.shape
    _, heads, positions, size = keys.shape
    chunk = 8
    cache_spec = pl.BlockSpec((chunk, heads, positions, size), lambda i, n: (i, 0, 0, 0))
    return pl.pallas_call(
        past_kernel,
        grid_spec=pltpu.PrefetchScalarGridSpec(
            num_scalar_prefetch=1,
            grid=(seqs // chunk,),
            in_specs=[
                pl.BlockSpec((steps, chunk, width), lambda i, n: (0, i, 0)),
                cache_spec,
                cache_spec,
            ],
            out_specs=[
                pl.BlockSpec((steps, chunk, width), lambda i, n: (0, i, 0)),
                pl.BlockSpec((steps, chunk, width), lambda i, n: (0, i, 0)),
            ],
        ),
        out_shape=[
            jax.ShapeDtypeStruct((steps, seqs, width), F32),
            jax.ShapeDtypeStruct((steps, seqs, width), F32),
        ],
        compiler_params=params(16),
        cost_estimate=cost(0, 4096),
        name="past",
    )(lengths, queries, keys, values)


def slot_mask(entries, rank, slots):
    return lax.div(iota((entries * rank, slots.shape[1]), 0), jnp.int32(rank)) == slots


def shrink_kernel(count, steps, cap, entries, rank, weight_ref, *refs):
    blocks, out_ref, slot_ref = refs[:count], refs[count], refs[count + 1]
    tiles = weight_ref.shape[1] // LANES
    rows = []
    for block in blocks:
        for s in range(steps):
            places = [(s * tiles + c) * cap for c in range(tiles)]
            rows.append(jnp.concatenate([block[p : p + cap, :] for p in places], axis=1))
    rows = jnp.concatenate(rows, axis=0)
    slots = [b[steps * tiles * cap :, :][:1, : steps * cap].astype(F32) for b in blocks]
    slots = jnp.concatenate(slots, axis=1).astype(jnp.int32)
    slot_ref[...] = slots
    every = lax.dot_general(weight_ref[...], rows, NT, preferred_element_type=F32)
    kept = jnp.where(slot_mask(entries, rank, slots), every, 0.0)
    out_ref[...] = jnp.sum(kept.reshape(entries, rank, kept.shape[1]), axis=0)


def shrink(weight, blocks, steps, cap):
    entries, rank, features = weight.shape
    count = len(blocks)
    rows = count * steps * cap
    return pl.pallas_call(
        functools.partial(shrink_kernel, count, steps, cap, entries, rank),
        out_shape=[
            jax.ShapeDtypeStruct((rank, rows), F32),
            jax.ShapeDtypeStruct((1, rows), jnp.int32),
        ],
        compiler_params=params(12),
        cost_estimate=cost(
            2 * entries * rank * features * rows, 2 * features * (entries * rank + rows)
        ),
        name="shrink",
    )(weight.reshape(entries * rank, features), *blocks)


def expand_kernel(groups, size, entries, rank, weight_ref, slot_ref, *refs):
    parts, outs = refs[:size], refs[size:]
    total = parts[0][...]
    for part in parts[1:]:
        total = total + part[...]
    shrunk = total.astype(BF16).astype(F32)
    spread = jnp.broadcast_to(shrunk[None], (entries,) + shrunk.shape).reshape(
        entries * rank, shrunk.shape[1]
    )
    spread = jnp.where(slot_mask(entries, rank, slot_ref[...]), spread, 0.0).astype(BF16)
    delta = adapter_scale * lax.dot_general(
        spread, weight_ref[...], TN, preferred_element_type=F32
    )
    delta = delta.astype(BF16)
    rows = outs[0].shape[0]
    for k in range(groups):
        outs[k][...] = delta[k * rows : (k + 1) * rows]


def expand(weight, parts, slots, groups):
    entries, rank, columns = weight.shape
    rows = parts[0].shape[1] // groups
    return pl.pallas_call(
        functools.partial(expand_kernel, groups, len(parts), entries, rank),
        out_shape=[jax.ShapeDtypeStruct((rows, columns), BF16)] * groups,
        compiler_params=params(8),
        cost_estimate=cost(
            2 * entries * rank * columns * rows * groups, 2 * entries * rank * columns
        ),
        name="expand",
    )(weight.reshape(entries * rank, columns), slots, *parts)


def finish_kernel(
    groups, size, cap, heads, back_ref, query_ref, mixed_ref, lse_ref, *refs
):
    summands, deltas = refs[:size], refs[size : size + groups]
    out_ref, new_ref = refs[size + groups :]
    steps, seqs, width = query_ref.shape
    columns = new_ref.shape[2]
    size = columns // (2 * heads)
    share = width // (size * heads)
    scaling = 1.0 / math.sqrt(size)
    back = back_ref[...]
    new = []
    for s in range(steps):
        delta = jnp.concatenate([r[s * cap : (s + 1) * cap, :] for r in deltas], axis=0)
        update = jnp.dot(back, delta, preferred_element_type=F32)
        rows = slice(s * seqs, (s + 1) * seqs)
        base = summands[0][rows, :]
        for summand in summands[1:]:
            base = base + summand[rows, :].astype(F32)
        new.append((base + update).astype(BF16))
        new_ref[s] = new[s]
    ones = jnp.ones((2 * size, size), BF16)
    for g in range(heads):
        left = g * 2 * size
        keys = [n[:, left : left + size].astype(F32) * scaling for n in new]
        values = [n[:, left + size : left + 2 * size].astype(F32) for n in new]
        for s in range(steps):
            for h in range(share):
                lanes = slice((g * share + h) * size, (g * share + h + 1) * size)
                q = query_ref[s, :, lanes].astype(F32)
                halves = []
                for t in range(s + 1):
                    product = q * keys[t]
                    high = product.astype(BF16)
                    low = (product - high.astype(F32)).astype(BF16)
                    halves.append(jnp.concatenate([high, low], axis=1))
                halves = jnp.concatenate(halves, axis=0)
                scores = jnp.dot(halves, ones, preferred_element_type=F32)
                scores = [scores[t * seqs : (t + 1) * seqs] for t in range(s + 1)]
                lse = lse_ref[s, :, lanes]
                top = lse
                for score in scores:
                    top = jnp.maximum(top, score)
                old = jnp.exp(lse - top)
                total = old
                mixed = mixed_ref[s, :, lanes] * old
                for t in range(s + 1):
                    raised = jnp.exp(scores[t] - top)
                    total = total + raised
                    mixed = mixed + raised * values[t]
                out_ref[s, :, lanes] = (mixed / total).astype(BF16)


def finish(back, summands, queries, mixed, lse, deltas, cap, heads):
    steps, seqs, width = queries.shape
    columns = summands[0].shape[1]
    return pl.pallas_call(
        functools.partial(finish_kernel, len(deltas), len(summands), cap, heads),
        out_shape=[
            jax.ShapeDtypeStruct((steps, seqs, width), BF16),
            jax.ShapeDtypeStruct((steps, seqs, columns), BF16),
        ],
        compiler_params=params(16),
        cost_estimate=cost(
            4 * steps * seqs * width * steps * LANES,
            8 * steps * seqs * width + 8 * steps * seqs * columns,
            steps * seqs * width * 2,
        ),
        name="finish",
    )(back, queries, mixed, lse, *summands, *deltas)


def body(
    hidden,
    queries,
    projection,
    cached_key_rows,
    cached_value_rows,
    adapter_shrink_weight,
    adapter_expand_weight,
    requests,
    adapter_store_row,
    lengths,
):
    steps, seqs, features = hidden.shape
    groups = lax.axis_size("dp")
    size = lax.axis_size("tp")
    cap = seqs // 4
    entries = adapter_shrink_weight.shape[0]
    heads = cached_key_rows.shape[1]

    routed = route(requests, adapter_store_row, hidden, groups, cap, entries)
    blocks, back = routed[:groups], routed[groups]
    over_dp = [None] + [swap("dp", groups, k) for k in range(1, groups)]
    over_tp = [None] + [swap("tp", size, k) for k in range(1, size)]
    got = {k: over_dp[k](blocks[k]) for k in reversed(range(1, groups))}

    late_hidden, _ = lax.optimization_barrier((hidden, back))
    parts = base(late_hidden.reshape(steps * seqs, features), projection, size)
    summands = [parts[0]] + [over_tp[k](parts[k]) for k in reversed(range(1, size))]

    mixed, lse = past(lengths, queries, cached_key_rows, cached_value_rows)

    block, _ = lax.optimization_barrier((blocks[0], (lse, parts[0])))
    gathered = [block] + [got[k] for k in range(1, groups)]
    shrunk, slots = shrink(adapter_shrink_weight, gathered, steps, cap)
    parts = [shrunk] + [over_tp[k](shrunk) for k in range(1, size)]
    deltas = expand(adapter_expand_weight, parts, slots, groups)
    deltas = [deltas[0]] + [over_dp[k](deltas[k]) for k in range(1, groups)]
    return tuple(finish(back, summands, queries, mixed, lse, deltas, cap, heads))


def solution(mesh):
    placed = (
        P(None, ("rep", "dp"), "tp"),
        P(None, ("rep", "dp"), "tp"),
        P("tp", None),
        P(("rep", "dp"), "tp", None, None),
        P(("rep", "dp"), "tp", None, None),
        P("dp", None, "tp"),
        P("dp", None, "tp"),
        P(("rep", "dp")),
        P("rep"),
        P(("rep", "dp")),
    )
    return jax.shard_map(
        body,
        mesh=mesh,
        in_specs=placed,
        out_specs=(P(None, ("rep", "dp"), "tp"), P(None, ("rep", "dp"), "tp")),
        check_vma=False,
    )
```

```python
import functools
import math

import jax
import jax.numpy as jnp
from jax import lax
from jax.experimental import pallas as pl
from jax.experimental.pallas import tpu as pltpu
from jax.sharding import PartitionSpec as P

adapter_scale = 0.5
F32 = jnp.float32
BF16 = jnp.bfloat16
NT = (((1,), (1,)), ((), ()))
TN = (((0,), (0,)), ((), ()))
MIB = 1024 * 1024
LANES = 128


def params(mib):
    return pltpu.CompilerParams(vmem_limit_bytes=mib * MIB)


def cost(flops, nbytes, transcendentals=0):
    return pl.CostEstimate(
        flops=int(flops), bytes_accessed=int(nbytes), transcendentals=int(transcendentals)
    )


def swap(axis, size, distance):
    pairs = [(i, i ^ distance) for i in range(size)]
    return lambda value: lax.ppermute(value, axis, pairs)


def iota(shape, dim):
    return lax.broadcasted_iota(jnp.int32, shape, dim)


def column(row):
    size = row.shape[1]
    diagonal = iota((size, size), 0) == iota((size, size), 1)
    return jnp.sum(jnp.where(diagonal, row, 0.0), axis=1, keepdims=True)


def route_kernel(order, cap, entries, requests_hbm, store_hbm, hidden_hbm, *refs):
    groups = len(order)
    blocks, back_ref = refs[:groups], refs[groups]
    requests_ref, store_ref, hidden_ref, index_sems, hidden_sems = refs[groups + 1 :]
    steps, seqs, features = hidden_ref.shape
    tiles = features // LANES
    index_copies = [
        pltpu.make_async_copy(requests_hbm, requests_ref, index_sems.at[0]),
        pltpu.make_async_copy(store_hbm, store_ref, index_sems.at[1]),
    ]
    hidden_copies = [
        pltpu.make_async_copy(hidden_hbm.at[s], hidden_ref.at[s], hidden_sems.at[s])
        for s in range(steps)
    ]
    for copy in index_copies + hidden_copies:
        copy.start()
    me = lax.axis_index("dp")
    for copy in index_copies:
        copy.wait()
    store_col = column(store_ref[...].astype(F32))
    adapters = store_col.shape[0]
    rows = jnp.sum(
        jnp.where(iota((adapters, seqs), 0) == requests_ref[...], store_col, 0.0),
        axis=0,
        keepdims=True,
    ).astype(jnp.int32)
    owner = lax.div(rows, jnp.int32(entries))
    slot_col = column((rows - owner * entries).astype(F32))
    distance = jnp.bitwise_xor(owner, me)
    turn = jnp.zeros(distance.shape, F32)
    for k, at in enumerate(order):
        turn = jnp.where(distance == at, float(k), turn)
    turn_col = column(turn)
    before = (turn_col == turn) & (iota((seqs, seqs), 0) < iota((seqs, seqs), 1))
    rank = jnp.sum(jnp.where(before, 1.0, 0.0), axis=0, keepdims=True)
    bucket = turn * cap + rank
    bucket_col = column(bucket).astype(jnp.int32)
    bucket = bucket.astype(jnp.int32)
    placed = jnp.where(iota((groups * cap, seqs), 0) == bucket, 1.0, 0.0).astype(BF16)
    back_ref[...] = jnp.where(bucket_col == iota((seqs, groups * cap), 1), 1.0, 0.0).astype(BF16)
    for k in range(groups):
        spot = lax.rem(iota((seqs, LANES), 1), jnp.int32(cap)) + k * cap
        slots = jnp.sum(jnp.where(bucket_col == spot, slot_col, 0.0), axis=0, keepdims=True)
        blocks[k][steps * tiles * cap :, :] = jnp.broadcast_to(slots, (cap, LANES)).astype(BF16)
    for s in range(steps):
        hidden_copies[s].wait()
        picked = jnp.dot(placed, hidden_ref[s], preferred_element_type=F32).astype(BF16)
        for k in range(groups):
            for c in range(tiles):
                first = (s * tiles + c) * cap
                blocks[k][first : first + cap, :] = picked[
                    k * cap : (k + 1) * cap, c * LANES : (c + 1) * LANES
                ]


def route(requests, store, hidden, order, cap, entries):
    groups = len(order)
    steps, seqs, features = hidden.shape
    rows = (steps * (features // LANES) + 1) * cap
    return pl.pallas_call(
        functools.partial(route_kernel, order, cap, entries),
        out_shape=[jax.ShapeDtypeStruct((rows, LANES), BF16)] * groups
        + [jax.ShapeDtypeStruct((seqs, groups * cap), BF16)],
        in_specs=[pl.BlockSpec(memory_space=pltpu.HBM)] * 3,
        scratch_shapes=[
            pltpu.VMEM((1, seqs), jnp.int32),
            pltpu.VMEM((1, store.shape[0]), jnp.int32),
            pltpu.VMEM(hidden.shape, BF16),
            pltpu.SemaphoreType.DMA((2,)),
            pltpu.SemaphoreType.DMA((steps,)),
        ],
        compiler_params=params(62),
        cost_estimate=cost(
            2 * groups * cap * seqs * steps * features, 4 * steps * seqs * features
        ),
        name="route",
    )(requests[None, :], store[None, :], hidden)


def base_kernel(size, hidden_ref, projection_ref, *outs):
    width = outs[0].shape[1]
    half = size // 2
    me = lax.axis_index("tp")
    for k in list(range(half, size)) + list(range(half)):
        first = pl.multiple_of(jnp.bitwise_xor(me, k) * width, width)
        part = jnp.dot(
            hidden_ref[...], projection_ref[:, pl.ds(first, width)], preferred_element_type=F32
        )
        outs[k][...] = part.astype(outs[k].dtype)


def base(hidden, projection, size):
    rows, _ = hidden.shape
    width = projection.shape[1] // size
    half = size // 2
    return pl.pallas_call(
        functools.partial(base_kernel, size),
        out_shape=[jax.ShapeDtypeStruct((rows, width), F32)] * half
        + [jax.ShapeDtypeStruct((rows, width), BF16)] * half,
        compiler_params=params(20),
        cost_estimate=cost(0, 4096),
        name="base",
    )(hidden, projection)


def past_kernel(lengths_ref, query_ref, key_ref, value_ref, mixed_ref, lse_ref):
    steps, chunk, width = query_ref.shape
    _, heads, positions, size = key_ref.shape
    share = width // (size * heads)
    rows = steps * share
    first = pl.program_id(0) * chunk
    scaling = 1.0 / math.sqrt(size)

    @pl.when(first == 0)
    def _():
        lse_ref[...] = jnp.zeros_like(lse_ref)

    def lanes(g, h):
        return slice((g * share + h) * size, (g * share + h + 1) * size)

    by_seq = {}
    for s in range(steps):
        whole = query_ref[s].astype(F32)
        for g in range(heads):
            stacked = jnp.stack([whole[:, lanes(g, h)] for h in range(share)], axis=0)
            by_seq[s, g] = jnp.swapaxes(stacked, 0, 1)
    units = [(i, g) for i in range(chunk) for g in range(heads)]
    scores = []
    for i, g in units:
        q = jnp.concatenate([by_seq[s, g][i] for s in range(steps)], axis=0).astype(BF16)
        raw = lax.dot_general(q, key_ref[i, g], NT, preferred_element_type=F32) * scaling
        live = iota((rows, positions), 1) < lengths_ref[first + i]
        scores.append(jnp.where(live, raw, -jnp.inf))
    scores = jnp.concatenate(scores, axis=0)
    top = jnp.max(scores, axis=1, keepdims=True)
    raised = jnp.exp(scores - top)
    total = jnp.sum(raised, axis=1, keepdims=True)
    weights = raised.astype(BF16)
    mixed = [
        jnp.dot(weights[u * rows : (u + 1) * rows], value_ref[i, g], preferred_element_type=F32)
        for u, (i, g) in enumerate(units)
    ]
    mixed = jnp.concatenate(mixed, axis=0) * (1.0 / total)
    lse = top + jnp.log(total)
    seqs = pl.num_programs(0) * chunk
    lane = lax.rem(iota((rows, LANES), 1), seqs)
    for g in range(heads):
        packed = lse_ref[g * rows : (g + 1) * rows, :]
        for i in range(chunk):
            u = i * heads + g
            packed = jnp.where(lane == first + i, lse[u * rows : (u + 1) * rows], packed)
        lse_ref[g * rows : (g + 1) * rows, :] = packed
    mixed = mixed.reshape(chunk, heads, steps, share, size)
    for s in range(steps):
        for g in range(heads):
            mixed_by_head = jnp.swapaxes(mixed[:, g, s], 0, 1)
            for h in range(share):
                mixed_ref[s, :, lanes(g, h)] = mixed_by_head[h]


def past(lengths, queries, keys, values):
    steps, seqs, width = queries.shape
    _, heads, positions, size = keys.shape
    chunk = 8
    cache_spec = pl.BlockSpec((chunk, heads, positions, size), lambda i, n: (i, 0, 0, 0))
    return pl.pallas_call(
        past_kernel,
        grid_spec=pltpu.PrefetchScalarGridSpec(
            num_scalar_prefetch=1,
            grid=(seqs // chunk,),
            in_specs=[
                pl.BlockSpec((steps, chunk, width), lambda i, n: (0, i, 0)),
                cache_spec,
                cache_spec,
            ],
            out_specs=[
                pl.BlockSpec((steps, chunk, width), lambda i, n: (0, i, 0)),
                pl.BlockSpec((steps * width // size, LANES), lambda i, n: (0, 0)),
            ],
        ),
        out_shape=[
            jax.ShapeDtypeStruct((steps, seqs, width), F32),
            jax.ShapeDtypeStruct((steps * width // size, LANES), F32),
        ],
        compiler_params=params(16),
        cost_estimate=cost(0, 4096),
        name="past",
    )(lengths, queries, keys, values)


def slot_mask(entries, rank, slots):
    return lax.div(iota((entries * rank, slots.shape[1]), 0), jnp.int32(rank)) == slots


def shrink_kernel(count, steps, cap, entries, rank, weight_ref, *refs):
    blocks, out_ref, slot_ref = refs[:count], refs[count], refs[count + 1]
    tiles = weight_ref.shape[1] // LANES
    rows = []
    for block in blocks:
        for s in range(steps):
            places = [(s * tiles + c) * cap for c in range(tiles)]
            rows.append(jnp.concatenate([block[p : p + cap, :] for p in places], axis=1))
    rows = jnp.concatenate(rows, axis=0)
    slots = [b[steps * tiles * cap :, :][:1, : steps * cap].astype(F32) for b in blocks]
    slots = jnp.concatenate(slots, axis=1).astype(jnp.int32)
    slot_ref[...] = slots
    every = lax.dot_general(weight_ref[...], rows, NT, preferred_element_type=F32)
    kept = jnp.where(slot_mask(entries, rank, slots), every, 0.0)
    out_ref[...] = jnp.sum(kept.reshape(entries, rank, kept.shape[1]), axis=0)


def shrink(weight, blocks, steps, cap):
    entries, rank, features = weight.shape
    count = len(blocks)
    rows = count * steps * cap
    return pl.pallas_call(
        functools.partial(shrink_kernel, count, steps, cap, entries, rank),
        out_shape=[
            jax.ShapeDtypeStruct((rank, rows), F32),
            jax.ShapeDtypeStruct((1, rows), jnp.int32),
        ],
        compiler_params=params(12),
        cost_estimate=cost(
            2 * entries * rank * features * rows, 2 * features * (entries * rank + rows)
        ),
        name="shrink",
    )(weight.reshape(entries * rank, features), *blocks)


def expand_kernel(groups, size, entries, rank, weight_ref, slot_ref, *refs):
    parts, outs = refs[:size], refs[size:]
    total = parts[0][...]
    for part in parts[1:]:
        total = total + part[...]
    shrunk = total.astype(BF16).astype(F32)
    spread = jnp.broadcast_to(shrunk[None], (entries,) + shrunk.shape).reshape(
        entries * rank, shrunk.shape[1]
    )
    spread = jnp.where(slot_mask(entries, rank, slot_ref[...]), spread, 0.0).astype(BF16)
    delta = adapter_scale * lax.dot_general(
        spread, weight_ref[...], TN, preferred_element_type=F32
    )
    delta = delta.astype(BF16)
    rows = outs[0].shape[0]
    for k in range(groups):
        outs[k][...] = delta[k * rows : (k + 1) * rows]


def expand(weight, parts, slots, groups):
    entries, rank, columns = weight.shape
    rows = parts[0].shape[1] // groups
    return pl.pallas_call(
        functools.partial(expand_kernel, groups, len(parts), entries, rank),
        out_shape=[jax.ShapeDtypeStruct((rows, columns), BF16)] * groups,
        compiler_params=params(8),
        cost_estimate=cost(
            2 * entries * rank * columns * rows * groups, 2 * entries * rank * columns
        ),
        name="expand",
    )(weight.reshape(entries * rank, columns), slots, *parts)


def finish_kernel(
    groups, size, cap, heads, back_ref, query_ref, mixed_ref, lse_ref, *refs
):
    summands, deltas = refs[:size], refs[size : size + groups]
    out_ref, new_ref = refs[size + groups :]
    steps, seqs, width = query_ref.shape
    columns = new_ref.shape[2]
    size = columns // (2 * heads)
    share = width // (size * heads)
    scaling = 1.0 / math.sqrt(size)
    back = back_ref[...]
    new = []
    for s in range(steps):
        delta = jnp.concatenate([r[s * cap : (s + 1) * cap, :] for r in deltas], axis=0)
        update = jnp.dot(back, delta, preferred_element_type=F32)
        rows = slice(s * seqs, (s + 1) * seqs)
        base = summands[0][rows, :]
        for summand in summands[1:]:
            base = base + summand[rows, :].astype(F32)
        new.append((base + update).astype(BF16))
        new_ref[s] = new[s]
    same = lax.rem(iota((seqs, LANES), 1), jnp.int32(seqs)) == iota((seqs, LANES), 0)

    def over_steps(parts, combine):
        whole = functools.reduce(combine, parts)
        turned = [pltpu.roll(whole, shift, 1) for shift in range(seqs, LANES, seqs)]
        return functools.reduce(combine, turned, whole)

    for g in range(heads):
        left = g * 2 * size
        keys = jnp.concatenate([n[:, left : left + size] for n in new], axis=0)
        values = jnp.concatenate([n[:, left + size : left + 2 * size] for n in new], axis=0)
        for s in range(steps):
            lanes = [
                slice((g * share + h) * size, (g * share + h + 1) * size) for h in range(share)
            ]
            count = pl.cdiv((s + 1) * seqs, LANES)
            q = jnp.concatenate([query_ref[s, :, cut] for cut in lanes], axis=0)
            scores = lax.dot_general(
                q, keys[: count * LANES], NT, preferred_element_type=F32
            )
            fresh = []
            for c in range(count):
                block = scores[:, c * LANES : (c + 1) * LANES].reshape(share, seqs, LANES)
                row = jnp.sum(jnp.where(same[None], block, 0.0), axis=1) * scaling
                step = lax.div(iota((share, LANES), 1), jnp.int32(seqs)) + c * (LANES // seqs)
                fresh.append(jnp.where(step <= s, row, -jnp.inf))
            first = (g * steps + s) * share
            lse = lse_ref[first : first + share, :]
            top = jnp.maximum(over_steps(fresh, jnp.maximum), lse)
            old = jnp.exp(lse - top)
            raised = [jnp.exp(row - top) for row in fresh]
            scale = 1.0 / (over_steps(raised, jnp.add) + old)
            old = jnp.transpose(old * scale)[:seqs, :]
            weights = jnp.concatenate(
                [
                    jnp.concatenate(
                        [
                            jnp.where(same, (row * scale)[h : h + 1, :], 0.0).astype(BF16)
                            for row in raised
                        ],
                        axis=1,
                    )
                    for h in range(share)
                ],
                axis=0,
            )
            mixed = jnp.dot(weights, values[: count * LANES], preferred_element_type=F32)
            for h in range(share):
                total = mixed[h * seqs : (h + 1) * seqs]
                total = total + mixed_ref[s, :, lanes[h]] * old[:, h : h + 1]
                out_ref[s, :, lanes[h]] = total.astype(BF16)


def finish(back, summands, queries, mixed, lse, deltas, cap, heads):
    steps, seqs, width = queries.shape
    columns = summands[0].shape[1]
    return pl.pallas_call(
        functools.partial(finish_kernel, len(deltas), len(summands), cap, heads),
        out_shape=[
            jax.ShapeDtypeStruct((steps, seqs, width), BF16),
            jax.ShapeDtypeStruct((steps, seqs, columns), BF16),
        ],
        compiler_params=params(16),
        cost_estimate=cost(
            4 * steps * seqs * width * steps * LANES,
            8 * steps * seqs * width + 8 * steps * seqs * columns,
            steps * seqs * width * 2,
        ),
        name="finish",
    )(back, queries, mixed, lse, *summands, *deltas)


def body(
    hidden,
    queries,
    projection,
    cached_key_rows,
    cached_value_rows,
    adapter_shrink_weight,
    adapter_expand_weight,
    requests,
    adapter_store_row,
    lengths,
):
    steps, seqs, features = hidden.shape
    groups = lax.axis_size("dp")
    size = lax.axis_size("tp")
    cap = seqs // 4
    entries = adapter_shrink_weight.shape[0]
    heads = cached_key_rows.shape[1]

    order = [0] + sorted(range(1, groups), key=lambda k: -k.bit_length())
    *blocks, back = route(requests, adapter_store_row, hidden, order, cap, entries)
    over_dp = [swap("dp", groups, k) for k in order[1:]]
    over_tp = [swap("tp", size, k) for k in range(1, size)]
    got = [move(block) for move, block in zip(over_dp, blocks[1:])]

    late_hidden, _ = lax.optimization_barrier((hidden, back))
    terms = base(late_hidden.reshape(steps * seqs, features), projection, size)
    distance = size // 2
    move = swap("tp", size, distance)
    terms = [[terms[k], move(terms[distance + k])] for k in range(distance)]

    mixed, lse = past(lengths, queries, cached_key_rows, cached_value_rows)

    block, _ = lax.optimization_barrier((blocks[0], lse))
    shrunk, slots = shrink(adapter_shrink_weight, [block] + got, steps, cap)
    partial = [shrunk] + [move(shrunk) for move in over_tp]
    terms, _ = lax.optimization_barrier((terms, shrunk))
    while distance > 1:
        distance //= 2
        move = swap("tp", size, distance)
        for k in range(distance):
            moved = sum(term.astype(F32) for term in terms[distance + k]).astype(BF16)
            terms[k] = terms[k] + [move(moved)]
    slots, _ = lax.optimization_barrier((slots, moved))
    deltas = expand(adapter_expand_weight, partial, slots, groups)
    returned = [deltas[0]] + [move(delta) for move, delta in zip(over_dp, deltas[1:])]
    summands = terms[0]
    return tuple(finish(back, summands, queries, mixed, lse, returned, cap, heads))


def solution(mesh):
    placed = (
        P(None, ("rep", "dp"), "tp"),
        P(None, ("rep", "dp"), "tp"),
        P("tp", None),
        P(("rep", "dp"), "tp", None, None),
        P(("rep", "dp"), "tp", None, None),
        P("dp", None, "tp"),
        P("dp", None, "tp"),
        P(("rep", "dp")),
        P("rep"),
        P(("rep", "dp")),
    )
    return jax.shard_map(
        body,
        mesh=mesh,
        in_specs=placed,
        out_specs=(P(None, ("rep", "dp"), "tp"), P(None, ("rep", "dp"), "tp")),
        check_vma=False,
    )
```

```python
import functools
import math

import jax
import jax.numpy as jnp
from jax import lax
from jax.experimental import pallas as pl
from jax.experimental.pallas import tpu as pltpu
from jax.sharding import PartitionSpec as P

adapter_scale = 0.5
F32 = jnp.float32
BF16 = jnp.bfloat16
NT = (((1,), (1,)), ((), ()))
TN = (((0,), (0,)), ((), ()))
MIB = 1024 * 1024
LANES = 128
BASE_MIB = 53


def params(mib):
    return pltpu.CompilerParams(vmem_limit_bytes=mib * MIB)


def cost(flops, nbytes, transcendentals=0):
    return pl.CostEstimate(
        flops=int(flops), bytes_accessed=int(nbytes), transcendentals=int(transcendentals)
    )


def swap(axis, size, distance):
    pairs = [(i, i ^ distance) for i in range(size)]
    return lambda value: lax.ppermute(value, axis, pairs)


def iota(shape, dim):
    return lax.broadcasted_iota(jnp.int32, shape, dim)


def column(row):
    size = row.shape[1]
    diagonal = iota((size, size), 0) == iota((size, size), 1)
    return jnp.sum(jnp.where(diagonal, row, 0.0), axis=1, keepdims=True)


def route_kernel(order, cap, entries, requests_hbm, store_hbm, hidden_hbm, *refs):
    groups = len(order)
    blocks, back_ref = refs[:groups], refs[groups]
    requests_ref, store_ref, hidden_ref, index_sems, hidden_sems = refs[groups + 1 :]
    steps, seqs, features = hidden_ref.shape
    tiles = features // LANES
    index_copies = [
        pltpu.make_async_copy(requests_hbm, requests_ref, index_sems.at[0]),
        pltpu.make_async_copy(store_hbm, store_ref, index_sems.at[1]),
    ]
    hidden_copies = [
        pltpu.make_async_copy(hidden_hbm.at[s], hidden_ref.at[s], hidden_sems.at[s])
        for s in range(steps)
    ]
    for copy in index_copies + hidden_copies:
        copy.start()
    me = lax.axis_index("dp")
    for copy in index_copies:
        copy.wait()
    store_col = column(store_ref[...].astype(F32))
    adapters = store_col.shape[0]
    rows = jnp.sum(
        jnp.where(iota((adapters, seqs), 0) == requests_ref[...], store_col, 0.0),
        axis=0,
        keepdims=True,
    ).astype(jnp.int32)
    owner = lax.div(rows, jnp.int32(entries))
    slot_col = column((rows - owner * entries).astype(F32))
    distance = jnp.bitwise_xor(owner, me)
    turn = jnp.zeros(distance.shape, F32)
    for k, at in enumerate(order):
        turn = jnp.where(distance == at, float(k), turn)
    turn_col = column(turn)
    before = (turn_col == turn) & (iota((seqs, seqs), 0) < iota((seqs, seqs), 1))
    rank = jnp.sum(jnp.where(before, 1.0, 0.0), axis=0, keepdims=True)
    bucket = turn * cap + rank
    bucket_col = column(bucket).astype(jnp.int32)
    bucket = bucket.astype(jnp.int32)
    placed = jnp.where(iota((groups * cap, seqs), 0) == bucket, 1.0, 0.0).astype(BF16)
    back_ref[...] = jnp.where(bucket_col == iota((seqs, groups * cap), 1), 1.0, 0.0).astype(BF16)
    for k in range(groups):
        spot = lax.rem(iota((seqs, LANES), 1), jnp.int32(cap)) + k * cap
        slots = jnp.sum(jnp.where(bucket_col == spot, slot_col, 0.0), axis=0, keepdims=True)
        blocks[k][steps * tiles * cap :, :] = jnp.broadcast_to(slots, (cap, LANES)).astype(BF16)
    for s in range(steps):
        hidden_copies[s].wait()
        picked = jnp.dot(placed, hidden_ref[s], preferred_element_type=F32).astype(BF16)
        for k in range(groups):
            for c in range(tiles):
                first = (s * tiles + c) * cap
                blocks[k][first : first + cap, :] = picked[
                    k * cap : (k + 1) * cap, c * LANES : (c + 1) * LANES
                ]


def route(requests, store, hidden, order, cap, entries):
    groups = len(order)
    steps, seqs, features = hidden.shape
    rows = (steps * (features // LANES) + 1) * cap
    return pl.pallas_call(
        functools.partial(route_kernel, order, cap, entries),
        out_shape=[jax.ShapeDtypeStruct((rows, LANES), BF16)] * groups
        + [jax.ShapeDtypeStruct((seqs, groups * cap), BF16)],
        in_specs=[pl.BlockSpec(memory_space=pltpu.HBM)] * 3,
        scratch_shapes=[
            pltpu.VMEM((1, seqs), jnp.int32),
            pltpu.VMEM((1, store.shape[0]), jnp.int32),
            pltpu.VMEM(hidden.shape, BF16),
            pltpu.SemaphoreType.DMA((2,)),
            pltpu.SemaphoreType.DMA((steps,)),
        ],
        compiler_params=params(62),
        cost_estimate=cost(
            2 * groups * cap * seqs * steps * features, 4 * steps * seqs * features
        ),
        name="route",
    )(requests[None, :], store[None, :], hidden)


def base_kernel(size, hidden_hbm, projection_hbm, *refs):
    outs, (hidden_ref, projection_ref, hidden_sem, block_sems) = refs[:size], refs[size:]
    width = outs[0].shape[1]
    half = size // 2
    me = lax.axis_index("tp")
    order = list(range(half, size)) + list(range(half))
    hidden_copy = pltpu.make_async_copy(hidden_hbm, hidden_ref, hidden_sem.at[0])
    hidden_copy.start()
    copies = {}
    for k in order:
        first = pl.multiple_of(jnp.bitwise_xor(me, k) * width, width)
        copies[k] = pltpu.make_async_copy(
            projection_hbm.at[:, pl.ds(first, width)], projection_ref.at[k], block_sems.at[k]
        )
        copies[k].start()
    hidden_copy.wait()
    for k in order:
        copies[k].wait()
        part = jnp.dot(hidden_ref[...], projection_ref[k], preferred_element_type=F32)
        outs[k][...] = part.astype(outs[k].dtype)


def base(hidden, projection, size):
    rows, features = hidden.shape
    width = projection.shape[1] // size
    half = size // 2
    return pl.pallas_call(
        functools.partial(base_kernel, size),
        out_shape=[jax.ShapeDtypeStruct((rows, width), F32)] * half
        + [jax.ShapeDtypeStruct((rows, width), BF16)] * half,
        in_specs=[pl.BlockSpec(memory_space=pltpu.HBM)] * 2,
        scratch_shapes=[
            pltpu.VMEM((rows, features), BF16),
            pltpu.VMEM((size, features, width), BF16),
            pltpu.SemaphoreType.DMA((1,)),
            pltpu.SemaphoreType.DMA((size,)),
        ],
        compiler_params=params(BASE_MIB),
        cost_estimate=cost(0, 4096),
        name="base",
    )(hidden, projection)


def past_kernel(lengths_ref, query_ref, key_ref, value_ref, mixed_ref, lse_ref):
    steps, chunk, width = query_ref.shape
    _, heads, positions, size = key_ref.shape
    share = width // (size * heads)
    rows = steps * share
    first = pl.program_id(0) * chunk
    scaling = 1.0 / math.sqrt(size)

    @pl.when(first == 0)
    def _():
        lse_ref[...] = jnp.zeros_like(lse_ref)

    def lanes(g, h):
        return slice((g * share + h) * size, (g * share + h + 1) * size)

    by_seq = {}
    for s in range(steps):
        whole = query_ref[s].astype(F32)
        for g in range(heads):
            stacked = jnp.stack([whole[:, lanes(g, h)] for h in range(share)], axis=0)
            by_seq[s, g] = jnp.swapaxes(stacked, 0, 1)
    units = [(i, g) for i in range(chunk) for g in range(heads)]
    scores = []
    for i, g in units:
        q = jnp.concatenate([by_seq[s, g][i] for s in range(steps)], axis=0).astype(BF16)
        raw = lax.dot_general(q, key_ref[i, g], NT, preferred_element_type=F32) * scaling
        live = iota((rows, positions), 1) < lengths_ref[first + i]
        scores.append(jnp.where(live, raw, -jnp.inf))
    scores = jnp.concatenate(scores, axis=0)
    top = jnp.max(scores, axis=1, keepdims=True)
    raised = jnp.exp(scores - top)
    total = jnp.sum(raised, axis=1, keepdims=True)
    weights = raised.astype(BF16)
    mixed = [
        jnp.dot(weights[u * rows : (u + 1) * rows], value_ref[i, g], preferred_element_type=F32)
        for u, (i, g) in enumerate(units)
    ]
    mixed = jnp.concatenate(mixed, axis=0) * (1.0 / total)
    lse = top + jnp.log(total)
    seqs = pl.num_programs(0) * chunk
    lane = lax.rem(iota((rows, LANES), 1), seqs)
    for g in range(heads):
        packed = lse_ref[g * rows : (g + 1) * rows, :]
        for i in range(chunk):
            u = i * heads + g
            packed = jnp.where(lane == first + i, lse[u * rows : (u + 1) * rows], packed)
        lse_ref[g * rows : (g + 1) * rows, :] = packed
    mixed = mixed.reshape(chunk, heads, steps, share, size)
    for s in range(steps):
        for g in range(heads):
            mixed_by_head = jnp.swapaxes(mixed[:, g, s], 0, 1)
            for h in range(share):
                mixed_ref[s, :, lanes(g, h)] = mixed_by_head[h]


def past(lengths, queries, keys, values):
    steps, seqs, width = queries.shape
    _, heads, positions, size = keys.shape
    chunk = 8
    cache_spec = pl.BlockSpec((chunk, heads, positions, size), lambda i, n: (i, 0, 0, 0))
    return pl.pallas_call(
        past_kernel,
        grid_spec=pltpu.PrefetchScalarGridSpec(
            num_scalar_prefetch=1,
            grid=(seqs // chunk,),
            in_specs=[
                pl.BlockSpec((steps, chunk, width), lambda i, n: (0, i, 0)),
                cache_spec,
                cache_spec,
            ],
            out_specs=[
                pl.BlockSpec((steps, chunk, width), lambda i, n: (0, i, 0)),
                pl.BlockSpec((steps * width // size, LANES), lambda i, n: (0, 0)),
            ],
        ),
        out_shape=[
            jax.ShapeDtypeStruct((steps, seqs, width), F32),
            jax.ShapeDtypeStruct((steps * width // size, LANES), F32),
        ],
        compiler_params=params(16),
        cost_estimate=cost(0, 4096),
        name="past",
    )(lengths, queries, keys, values)


def slot_mask(entries, rank, slots):
    return lax.div(iota((entries * rank, slots.shape[1]), 0), jnp.int32(rank)) == slots


def shrink_kernel(count, steps, cap, entries, rank, weight_ref, *refs):
    blocks, out_ref, slot_ref = refs[:count], refs[count], refs[count + 1]
    tiles = weight_ref.shape[1] // LANES
    rows = []
    for block in blocks:
        for s in range(steps):
            places = [(s * tiles + c) * cap for c in range(tiles)]
            rows.append(jnp.concatenate([block[p : p + cap, :] for p in places], axis=1))
    rows = jnp.concatenate(rows, axis=0)
    slots = [b[steps * tiles * cap :, :][:1, : steps * cap].astype(F32) for b in blocks]
    slots = jnp.concatenate(slots, axis=1).astype(jnp.int32)
    slot_ref[...] = slots
    every = lax.dot_general(weight_ref[...], rows, NT, preferred_element_type=F32)
    kept = jnp.where(slot_mask(entries, rank, slots), every, 0.0)
    out_ref[...] = jnp.sum(kept.reshape(entries, rank, kept.shape[1]), axis=0)


def shrink(weight, blocks, steps, cap):
    entries, rank, features = weight.shape
    count = len(blocks)
    rows = count * steps * cap
    return pl.pallas_call(
        functools.partial(shrink_kernel, count, steps, cap, entries, rank),
        out_shape=[
            jax.ShapeDtypeStruct((rank, rows), F32),
            jax.ShapeDtypeStruct((1, rows), jnp.int32),
        ],
        compiler_params=params(12),
        cost_estimate=cost(
            2 * entries * rank * features * rows, 2 * features * (entries * rank + rows)
        ),
        name="shrink",
    )(weight.reshape(entries * rank, features), *blocks)


def expand_kernel(groups, size, entries, rank, weight_ref, slot_ref, *refs):
    parts, outs = refs[:size], refs[size:]
    total = parts[0][...]
    for part in parts[1:]:
        total = total + part[...]
    shrunk = total.astype(BF16).astype(F32)
    spread = jnp.broadcast_to(shrunk[None], (entries,) + shrunk.shape).reshape(
        entries * rank, shrunk.shape[1]
    )
    spread = jnp.where(slot_mask(entries, rank, slot_ref[...]), spread, 0.0).astype(BF16)
    delta = adapter_scale * lax.dot_general(
        spread, weight_ref[...], TN, preferred_element_type=F32
    )
    delta = delta.astype(BF16)
    rows = outs[0].shape[0]
    for k in range(groups):
        outs[k][...] = delta[k * rows : (k + 1) * rows]


def expand(weight, parts, slots, groups):
    entries, rank, columns = weight.shape
    rows = parts[0].shape[1] // groups
    return pl.pallas_call(
        functools.partial(expand_kernel, groups, len(parts), entries, rank),
        out_shape=[jax.ShapeDtypeStruct((rows, columns), BF16)] * groups,
        compiler_params=params(8),
        cost_estimate=cost(
            2 * entries * rank * columns * rows * groups, 2 * entries * rank * columns
        ),
        name="expand",
    )(weight.reshape(entries * rank, columns), slots, *parts)


def finish_kernel(
    groups, size, cap, heads, back_ref, query_ref, mixed_ref, lse_ref, *refs
):
    summands, deltas = refs[:size], refs[size : size + groups]
    out_hbm, new_hbm, out_ref, new_ref, out_sems, new_sems = refs[size + groups :]
    steps, seqs, width = query_ref.shape
    columns = new_ref.shape[2]
    size = columns // (2 * heads)
    share = width // (size * heads)
    scaling = 1.0 / math.sqrt(size)
    back = back_ref[...]
    new = []
    copies = []
    for s in range(steps):
        delta = jnp.concatenate([r[s * cap : (s + 1) * cap, :] for r in deltas], axis=0)
        update = jnp.dot(back, delta, preferred_element_type=F32)
        rows = slice(s * seqs, (s + 1) * seqs)
        base = summands[0][rows, :]
        for summand in summands[1:]:
            base = base + summand[rows, :].astype(F32)
        new.append((base + update).astype(BF16))
        new_ref[s] = new[s]
        copies.append(pltpu.make_async_copy(new_ref.at[s], new_hbm.at[s], new_sems.at[s]))
        copies[-1].start()
    same = lax.rem(iota((seqs, LANES), 1), jnp.int32(seqs)) == iota((seqs, LANES), 0)

    def over_steps(parts, combine):
        whole = functools.reduce(combine, parts)
        turned = [pltpu.roll(whole, shift, 1) for shift in range(seqs, LANES, seqs)]
        return functools.reduce(combine, turned, whole)

    parts = steps * seqs // LANES
    rows = heads * steps * share
    units = [(g, s) for g in range(heads) for s in range(steps)]

    def lanes(g, h):
        return slice((g * share + h) * size, (g * share + h + 1) * size)

    fresh = [[] for _ in range(parts)]
    values = []
    for g in range(heads):
        left = g * 2 * size
        keys = jnp.concatenate([n[:, left : left + size] for n in new], axis=0)
        values.append(
            jnp.concatenate([n[:, left + size : left + 2 * size] for n in new], axis=0)
        )
        for s in range(steps):
            count = pl.cdiv((s + 1) * seqs, LANES)
            q = jnp.concatenate([query_ref[s, :, lanes(g, h)] for h in range(share)], axis=0)
            scores = lax.dot_general(q, keys[: count * LANES], NT, preferred_element_type=F32)
            for c in range(parts):
                if c < count:
                    block = scores[:, c * LANES : (c + 1) * LANES].reshape(share, seqs, LANES)
                    fresh[c].append(jnp.sum(jnp.where(same[None], block, 0.0), axis=1))
                else:
                    fresh[c].append(jnp.zeros((share, LANES), F32))
    now = lax.rem(lax.div(iota((rows, LANES), 0), jnp.int32(share)), jnp.int32(steps))
    step = lax.div(iota((rows, LANES), 1), jnp.int32(seqs))
    fresh = [
        jnp.where(
            step + c * (LANES // seqs) <= now,
            jnp.concatenate(fresh[c], axis=0) * scaling,
            -jnp.inf,
        )
        for c in range(parts)
    ]
    lse = lse_ref[...]
    top = jnp.maximum(over_steps(fresh, jnp.maximum), lse)
    old = jnp.exp(lse - top)
    raised = [jnp.exp(part - top) for part in fresh]
    scale = 1.0 / (over_steps(raised, jnp.add) + old)
    weights = [part * scale for part in raised]
    old = jnp.transpose(old * scale)[:seqs, :]
    for g, s in units:
        count = pl.cdiv((s + 1) * seqs, LANES)
        first = (g * steps + s) * share
        spread = []
        for h in range(share):
            row = slice(first + h, first + h + 1)
            spread.append(
                jnp.concatenate(
                    [jnp.where(same, weights[c][row], 0.0).astype(BF16) for c in range(count)],
                    axis=1,
                )
            )
        mixed = jnp.dot(
            jnp.concatenate(spread, axis=0),
            values[g][: count * LANES],
            preferred_element_type=F32,
        )
        for h in range(share):
            total = mixed[h * seqs : (h + 1) * seqs]
            total = total + mixed_ref[s, :, lanes(g, h)] * old[:, first + h : first + h + 1]
            out_ref[s, :, lanes(g, h)] = total.astype(BF16)
        part = (s, slice(None), pl.ds(g * share * size, share * size))
        copies.append(
            pltpu.make_async_copy(
                out_ref.at[part], out_hbm.at[part], out_sems.at[g * steps + s]
            )
        )
        copies[-1].start()
    for copy in copies:
        copy.wait()


def finish(back, summands, queries, mixed, lse, deltas, cap, heads):
    steps, seqs, width = queries.shape
    columns = summands[0].shape[1]
    return pl.pallas_call(
        functools.partial(finish_kernel, len(deltas), len(summands), cap, heads),
        out_shape=[
            jax.ShapeDtypeStruct((steps, seqs, width), BF16),
            jax.ShapeDtypeStruct((steps, seqs, columns), BF16),
        ],
        out_specs=[pl.BlockSpec(memory_space=pltpu.HBM)] * 2,
        scratch_shapes=[
            pltpu.VMEM((steps, seqs, width), BF16),
            pltpu.VMEM((steps, seqs, columns), BF16),
            pltpu.SemaphoreType.DMA((heads * steps,)),
            pltpu.SemaphoreType.DMA((steps,)),
        ],
        compiler_params=params(16),
        cost_estimate=cost(
            4 * steps * seqs * width * steps * LANES,
            8 * steps * seqs * width + 8 * steps * seqs * columns,
            steps * seqs * width * 2,
        ),
        name="finish",
    )(back, queries, mixed, lse, *summands, *deltas)


def body(
    hidden,
    queries,
    projection,
    cached_key_rows,
    cached_value_rows,
    adapter_shrink_weight,
    adapter_expand_weight,
    requests,
    adapter_store_row,
    lengths,
):
    steps, seqs, features = hidden.shape
    groups = lax.axis_size("dp")
    size = lax.axis_size("tp")
    cap = seqs // 4
    entries = adapter_shrink_weight.shape[0]
    heads = cached_key_rows.shape[1]

    order = [0] + sorted(range(1, groups), key=lambda k: -k.bit_length())
    *blocks, back = route(requests, adapter_store_row, hidden, order, cap, entries)
    over_dp = [swap("dp", groups, k) for k in order[1:]]
    over_tp = [swap("tp", size, k) for k in reversed(range(1, size))]
    got = [move(block) for move, block in zip(over_dp, blocks[1:])]

    late_hidden, _ = lax.optimization_barrier((hidden, back))
    terms = base(late_hidden.reshape(steps * seqs, features), projection, size)
    distance = size // 2
    move = swap("tp", size, distance)
    terms = [[terms[k], move(terms[distance + k])] for k in range(distance)]

    mixed, lse = past(lengths, queries, cached_key_rows, cached_value_rows)

    block, _ = lax.optimization_barrier((blocks[0], lse))
    shrunk, slots = shrink(adapter_shrink_weight, [block] + got, steps, cap)
    partial = [shrunk] + [move(shrunk) for move in over_tp]
    deltas = expand(adapter_expand_weight, partial, slots, groups)
    returned = [deltas[0]] + [move(delta) for move, delta in zip(over_dp, deltas[1:])]
    terms, _ = lax.optimization_barrier((terms, deltas[0]))
    while distance > 1:
        distance //= 2
        move = swap("tp", size, distance)
        for k in range(distance):
            moved = sum(term.astype(F32) for term in terms[distance + k]).astype(BF16)
            terms[k] = terms[k] + [move(moved)]
    summands = terms[0]
    return tuple(finish(back, summands, queries, mixed, lse, returned, cap, heads))


def solution(mesh):
    placed = (
        P(None, ("rep", "dp"), "tp"),
        P(None, ("rep", "dp"), "tp"),
        P("tp", None),
        P(("rep", "dp"), "tp", None, None),
        P(("rep", "dp"), "tp", None, None),
        P("dp", None, "tp"),
        P("dp", None, "tp"),
        P(("rep", "dp")),
        P("rep"),
        P(("rep", "dp")),
    )
    return jax.shard_map(
        body,
        mesh=mesh,
        in_specs=placed,
        out_specs=(P(None, ("rep", "dp"), "tp"), P(None, ("rep", "dp"), "tp")),
        check_vma=False,
    )
```

```python
import functools
import math

import jax
import jax.numpy as jnp
from jax import lax
from jax.experimental import pallas as pl
from jax.experimental.pallas import tpu as pltpu
from jax.sharding import PartitionSpec as P

adapter_scale = 0.5
F32 = jnp.float32
BF16 = jnp.bfloat16
NT = (((1,), (1,)), ((), ()))
TN = (((0,), (0,)), ((), ()))
MIB = 1024 * 1024
LANES = 128
BASE_MIB = 53


def params(mib):
    return pltpu.CompilerParams(vmem_limit_bytes=mib * MIB)


def cost(flops, nbytes, transcendentals=0):
    return pl.CostEstimate(
        flops=int(flops), bytes_accessed=int(nbytes), transcendentals=int(transcendentals)
    )


def swap(axis, size, distance):
    pairs = [(i, i ^ distance) for i in range(size)]
    return lambda value: lax.ppermute(value, axis, pairs)


def iota(shape, dim):
    return lax.broadcasted_iota(jnp.int32, shape, dim)


def column(row):
    size = row.shape[1]
    diagonal = iota((size, size), 0) == iota((size, size), 1)
    return jnp.sum(jnp.where(diagonal, row, 0.0), axis=1, keepdims=True)


def route_kernel(order, cap, entries, requests_hbm, store_hbm, hidden_hbm, *refs):
    groups = len(order)
    blocks, back_ref = refs[:groups], refs[groups]
    requests_ref, store_ref, hidden_ref, index_sems, hidden_sems = refs[groups + 1 :]
    steps, seqs, features = hidden_ref.shape
    tiles = features // LANES
    index_copies = [
        pltpu.make_async_copy(requests_hbm, requests_ref, index_sems.at[0]),
        pltpu.make_async_copy(store_hbm, store_ref, index_sems.at[1]),
    ]
    hidden_copies = [
        pltpu.make_async_copy(hidden_hbm.at[s], hidden_ref.at[s], hidden_sems.at[s])
        for s in range(steps)
    ]
    for copy in index_copies + hidden_copies:
        copy.start()
    me = lax.axis_index("dp")
    for copy in index_copies:
        copy.wait()
    store_col = column(store_ref[...].astype(F32))
    adapters = store_col.shape[0]
    rows = jnp.sum(
        jnp.where(iota((adapters, seqs), 0) == requests_ref[...], store_col, 0.0),
        axis=0,
        keepdims=True,
    ).astype(jnp.int32)
    owner = lax.div(rows, jnp.int32(entries))
    slot_col = column((rows - owner * entries).astype(F32))
    distance = jnp.bitwise_xor(owner, me)
    turn = jnp.zeros(distance.shape, F32)
    for k, at in enumerate(order):
        turn = jnp.where(distance == at, float(k), turn)
    turn_col = column(turn)
    before = (turn_col == turn) & (iota((seqs, seqs), 0) < iota((seqs, seqs), 1))
    rank = jnp.sum(jnp.where(before, 1.0, 0.0), axis=0, keepdims=True)
    bucket = turn * cap + rank
    bucket_col = column(bucket).astype(jnp.int32)
    bucket = bucket.astype(jnp.int32)
    placed = jnp.where(iota((groups * cap, seqs), 0) == bucket, 1.0, 0.0).astype(BF16)
    back_ref[...] = jnp.where(bucket_col == iota((seqs, groups * cap), 1), 1.0, 0.0).astype(BF16)
    for k in range(groups):
        spot = lax.rem(iota((seqs, LANES), 1), jnp.int32(cap)) + k * cap
        slots = jnp.sum(jnp.where(bucket_col == spot, slot_col, 0.0), axis=0, keepdims=True)
        blocks[k][steps * tiles * cap :, :] = jnp.broadcast_to(slots, (cap, LANES)).astype(BF16)
    for s in range(steps):
        hidden_copies[s].wait()
        picked = jnp.dot(placed, hidden_ref[s], preferred_element_type=F32).astype(BF16)
        for k in range(groups):
            for c in range(tiles):
                first = (s * tiles + c) * cap
                blocks[k][first : first + cap, :] = picked[
                    k * cap : (k + 1) * cap, c * LANES : (c + 1) * LANES
                ]


def route(requests, store, hidden, order, cap, entries):
    groups = len(order)
    steps, seqs, features = hidden.shape
    rows = (steps * (features // LANES) + 1) * cap
    return pl.pallas_call(
        functools.partial(route_kernel, order, cap, entries),
        out_shape=[jax.ShapeDtypeStruct((rows, LANES), BF16)] * groups
        + [jax.ShapeDtypeStruct((seqs, groups * cap), BF16)],
        in_specs=[pl.BlockSpec(memory_space=pltpu.HBM)] * 3,
        scratch_shapes=[
            pltpu.VMEM((1, seqs), jnp.int32),
            pltpu.VMEM((1, store.shape[0]), jnp.int32),
            pltpu.VMEM(hidden.shape, BF16),
            pltpu.SemaphoreType.DMA((2,)),
            pltpu.SemaphoreType.DMA((steps,)),
        ],
        compiler_params=params(62),
        cost_estimate=cost(
            2 * groups * cap * seqs * steps * features, 4 * steps * seqs * features
        ),
        name="route",
    )(requests[None, :], store[None, :], hidden)


def base_kernel(size, hidden_hbm, projection_hbm, *refs):
    outs, (hidden_ref, projection_ref, hidden_sem, block_sems) = refs[:size], refs[size:]
    width = outs[0].shape[1]
    half = size // 2
    me = lax.axis_index("tp")
    order = list(range(half, size)) + list(range(half))
    hidden_copy = pltpu.make_async_copy(hidden_hbm, hidden_ref, hidden_sem.at[0])
    hidden_copy.start()
    copies = {}
    for k in order:
        first = pl.multiple_of(jnp.bitwise_xor(me, k) * width, width)
        copies[k] = pltpu.make_async_copy(
            projection_hbm.at[:, pl.ds(first, width)], projection_ref.at[k], block_sems.at[k]
        )
        copies[k].start()
    hidden_copy.wait()
    for k in order:
        copies[k].wait()
        part = jnp.dot(hidden_ref[...], projection_ref[k], preferred_element_type=F32)
        outs[k][...] = part.astype(outs[k].dtype)


def base(hidden, projection, size):
    rows, features = hidden.shape
    width = projection.shape[1] // size
    half = size // 2
    return pl.pallas_call(
        functools.partial(base_kernel, size),
        out_shape=[jax.ShapeDtypeStruct((rows, width), F32)] * half
        + [jax.ShapeDtypeStruct((rows, width), BF16)] * half,
        in_specs=[pl.BlockSpec(memory_space=pltpu.HBM)] * 2,
        scratch_shapes=[
            pltpu.VMEM((rows, features), BF16),
            pltpu.VMEM((size, features, width), BF16),
            pltpu.SemaphoreType.DMA((1,)),
            pltpu.SemaphoreType.DMA((size,)),
        ],
        compiler_params=params(BASE_MIB),
        cost_estimate=cost(0, 4096),
        name="base",
    )(hidden, projection)


def past_kernel(lengths_ref, query_ref, key_ref, value_ref, mixed_ref, lse_ref):
    steps, chunk, width = query_ref.shape
    _, heads, positions, size = key_ref.shape
    share = width // (size * heads)
    rows = steps * share
    first = pl.program_id(0) * chunk
    scaling = 1.0 / math.sqrt(size)

    @pl.when(first == 0)
    def _():
        lse_ref[...] = jnp.zeros_like(lse_ref)

    def lanes(g, h):
        return slice((g * share + h) * size, (g * share + h + 1) * size)

    by_seq = {}
    for s in range(steps):
        whole = query_ref[s].astype(F32)
        for g in range(heads):
            stacked = jnp.stack([whole[:, lanes(g, h)] for h in range(share)], axis=0)
            by_seq[s, g] = jnp.swapaxes(stacked, 0, 1)
    units = [(i, g) for i in range(chunk) for g in range(heads)]
    scores = []
    for i, g in units:
        q = jnp.concatenate([by_seq[s, g][i] for s in range(steps)], axis=0).astype(BF16)
        raw = lax.dot_general(q, key_ref[i, g], NT, preferred_element_type=F32) * scaling
        live = iota((rows, positions), 1) < lengths_ref[first + i]
        scores.append(jnp.where(live, raw, -jnp.inf))
    scores = jnp.concatenate(scores, axis=0)
    top = jnp.max(scores, axis=1, keepdims=True)
    raised = jnp.exp(scores - top)
    total = jnp.sum(raised, axis=1, keepdims=True)
    weights = raised.astype(BF16)
    mixed = [
        jnp.dot(weights[u * rows : (u + 1) * rows], value_ref[i, g], preferred_element_type=F32)
        for u, (i, g) in enumerate(units)
    ]
    mixed = jnp.concatenate(mixed, axis=0) * (1.0 / total)
    lse = top + jnp.log(total)
    seqs = pl.num_programs(0) * chunk
    lane = lax.rem(iota((rows, LANES), 1), seqs)
    for g in range(heads):
        packed = lse_ref[g * rows : (g + 1) * rows, :]
        for i in range(chunk):
            u = i * heads + g
            packed = jnp.where(lane == first + i, lse[u * rows : (u + 1) * rows], packed)
        lse_ref[g * rows : (g + 1) * rows, :] = packed
    mixed = mixed.reshape(chunk, heads, steps, share, size)
    for s in range(steps):
        for g in range(heads):
            mixed_by_head = jnp.swapaxes(mixed[:, g, s], 0, 1)
            for h in range(share):
                mixed_ref[s, :, lanes(g, h)] = mixed_by_head[h]


def past(lengths, queries, keys, values):
    steps, seqs, width = queries.shape
    _, heads, positions, size = keys.shape
    chunk = 8
    cache_spec = pl.BlockSpec((chunk, heads, positions, size), lambda i, n: (i, 0, 0, 0))
    return pl.pallas_call(
        past_kernel,
        grid_spec=pltpu.PrefetchScalarGridSpec(
            num_scalar_prefetch=1,
            grid=(seqs // chunk,),
            in_specs=[
                pl.BlockSpec((steps, chunk, width), lambda i, n: (0, i, 0)),
                cache_spec,
                cache_spec,
            ],
            out_specs=[
                pl.BlockSpec((steps, chunk, width), lambda i, n: (0, i, 0)),
                pl.BlockSpec((steps * width // size, LANES), lambda i, n: (0, 0)),
            ],
        ),
        out_shape=[
            jax.ShapeDtypeStruct((steps, seqs, width), F32),
            jax.ShapeDtypeStruct((steps * width // size, LANES), F32),
        ],
        compiler_params=params(16),
        cost_estimate=cost(0, 4096),
        name="past",
    )(lengths, queries, keys, values)


def slot_mask(entries, rank, slots):
    return lax.div(iota((entries * rank, slots.shape[1]), 0), jnp.int32(rank)) == slots


def shrink_kernel(count, steps, cap, entries, rank, weight_ref, *refs):
    blocks, out_ref, slot_ref = refs[:count], refs[count], refs[count + 1]
    tiles = weight_ref.shape[1] // LANES
    rows = []
    for block in blocks:
        for s in range(steps):
            places = [(s * tiles + c) * cap for c in range(tiles)]
            rows.append(jnp.concatenate([block[p : p + cap, :] for p in places], axis=1))
    rows = jnp.concatenate(rows, axis=0)
    slots = [b[steps * tiles * cap :, :][:1, : steps * cap].astype(F32) for b in blocks]
    slots = jnp.concatenate(slots, axis=1).astype(jnp.int32)
    slot_ref[...] = slots
    every = lax.dot_general(weight_ref[...], rows, NT, preferred_element_type=F32)
    kept = jnp.where(slot_mask(entries, rank, slots), every, 0.0)
    out_ref[...] = jnp.sum(kept.reshape(entries, rank, kept.shape[1]), axis=0)


def shrink(weight, blocks, steps, cap):
    entries, rank, features = weight.shape
    count = len(blocks)
    rows = count * steps * cap
    return pl.pallas_call(
        functools.partial(shrink_kernel, count, steps, cap, entries, rank),
        out_shape=[
            jax.ShapeDtypeStruct((rank, rows), F32),
            jax.ShapeDtypeStruct((1, rows), jnp.int32),
        ],
        compiler_params=params(12),
        cost_estimate=cost(
            2 * entries * rank * features * rows, 2 * features * (entries * rank + rows)
        ),
        name="shrink",
    )(weight.reshape(entries * rank, features), *blocks)


def expand_kernel(groups, size, entries, rank, weight_ref, slot_ref, *refs):
    parts, outs = refs[:size], refs[size:]
    total = parts[0][...]
    for part in parts[1:]:
        total = total + part[...]
    shrunk = total.astype(BF16).astype(F32)
    spread = jnp.broadcast_to(shrunk[None], (entries,) + shrunk.shape).reshape(
        entries * rank, shrunk.shape[1]
    )
    spread = jnp.where(slot_mask(entries, rank, slot_ref[...]), spread, 0.0).astype(BF16)
    delta = adapter_scale * lax.dot_general(
        spread, weight_ref[...], TN, preferred_element_type=F32
    )
    delta = delta.astype(BF16)
    rows = outs[0].shape[0]
    for k in range(groups):
        outs[k][...] = delta[k * rows : (k + 1) * rows]


def expand(weight, parts, slots, groups):
    entries, rank, columns = weight.shape
    rows = parts[0].shape[1] // groups
    return pl.pallas_call(
        functools.partial(expand_kernel, groups, len(parts), entries, rank),
        out_shape=[jax.ShapeDtypeStruct((rows, columns), BF16)] * groups,
        compiler_params=params(8),
        cost_estimate=cost(
            2 * entries * rank * columns * rows * groups, 2 * entries * rank * columns
        ),
        name="expand",
    )(weight.reshape(entries * rank, columns), slots, *parts)


def finish_kernel(
    turns, size, cap, heads, back_ref, query_ref, mixed_ref, lse_ref, *refs
):
    groups = len(turns)
    summands = refs[:size]
    deltas = [refs[size + turns.index(k)] for k in range(groups)]
    out_hbm, new_hbm, out_ref, new_ref, out_sems, new_sems = refs[size + groups :]
    steps, seqs, width = query_ref.shape
    columns = new_ref.shape[2]
    size = columns // (2 * heads)
    share = width // (size * heads)
    scaling = 1.0 / math.sqrt(size)
    back = back_ref[...]
    new = []
    copies = []
    for s in range(steps):
        delta = jnp.concatenate([r[s * cap : (s + 1) * cap, :] for r in deltas], axis=0)
        update = jnp.dot(back, delta, preferred_element_type=F32)
        rows = slice(s * seqs, (s + 1) * seqs)
        base = summands[0][rows, :]
        for summand in summands[1:]:
            base = base + summand[rows, :].astype(F32)
        new.append((base + update).astype(BF16))
        new_ref[s] = new[s]
        copies.append(pltpu.make_async_copy(new_ref.at[s], new_hbm.at[s], new_sems.at[s]))
        copies[-1].start()
    same = lax.rem(iota((seqs, LANES), 1), jnp.int32(seqs)) == iota((seqs, LANES), 0)

    def over_steps(parts, combine):
        whole = functools.reduce(combine, parts)
        turned = [pltpu.roll(whole, shift, 1) for shift in range(seqs, LANES, seqs)]
        return functools.reduce(combine, turned, whole)

    parts = steps * seqs // LANES
    rows = heads * steps * share
    units = [(g, s) for g in range(heads) for s in range(steps)]

    def lanes(g, h):
        return slice((g * share + h) * size, (g * share + h + 1) * size)

    fresh = [[] for _ in range(parts)]
    values = []
    for g in range(heads):
        left = g * 2 * size
        keys = jnp.concatenate([n[:, left : left + size] for n in new], axis=0)
        values.append(
            jnp.concatenate([n[:, left + size : left + 2 * size] for n in new], axis=0)
        )
        for s in range(steps):
            count = pl.cdiv((s + 1) * seqs, LANES)
            q = jnp.concatenate([query_ref[s, :, lanes(g, h)] for h in range(share)], axis=0)
            scores = lax.dot_general(q, keys[: count * LANES], NT, preferred_element_type=F32)
            for c in range(parts):
                if c < count:
                    block = scores[:, c * LANES : (c + 1) * LANES].reshape(share, seqs, LANES)
                    fresh[c].append(jnp.sum(jnp.where(same[None], block, 0.0), axis=1))
                else:
                    fresh[c].append(jnp.zeros((share, LANES), F32))
    now = lax.rem(lax.div(iota((rows, LANES), 0), jnp.int32(share)), jnp.int32(steps))
    step = lax.div(iota((rows, LANES), 1), jnp.int32(seqs))
    fresh = [
        jnp.where(
            step + c * (LANES // seqs) <= now,
            jnp.concatenate(fresh[c], axis=0) * scaling,
            -jnp.inf,
        )
        for c in range(parts)
    ]
    lse = lse_ref[...]
    top = jnp.maximum(over_steps(fresh, jnp.maximum), lse)
    old = jnp.exp(lse - top)
    raised = [jnp.exp(part - top) for part in fresh]
    scale = 1.0 / (over_steps(raised, jnp.add) + old)
    weights = [part * scale for part in raised]
    old = jnp.transpose(old * scale)[:seqs, :]
    for g, s in units:
        count = pl.cdiv((s + 1) * seqs, LANES)
        first = (g * steps + s) * share
        spread = []
        for h in range(share):
            row = slice(first + h, first + h + 1)
            spread.append(
                jnp.concatenate(
                    [jnp.where(same, weights[c][row], 0.0).astype(BF16) for c in range(count)],
                    axis=1,
                )
            )
        mixed = jnp.dot(
            jnp.concatenate(spread, axis=0),
            values[g][: count * LANES],
            preferred_element_type=F32,
        )
        for h in range(share):
            total = mixed[h * seqs : (h + 1) * seqs]
            total = total + mixed_ref[s, :, lanes(g, h)] * old[:, first + h : first + h + 1]
            out_ref[s, :, lanes(g, h)] = total.astype(BF16)
        part = (s, slice(None), pl.ds(g * share * size, share * size))
        copies.append(
            pltpu.make_async_copy(
                out_ref.at[part], out_hbm.at[part], out_sems.at[g * steps + s]
            )
        )
        copies[-1].start()
    for copy in copies:
        copy.wait()


def finish(back, summands, queries, mixed, lse, deltas, turns, cap, heads):
    steps, seqs, width = queries.shape
    columns = summands[0].shape[1]
    return pl.pallas_call(
        functools.partial(finish_kernel, turns, len(summands), cap, heads),
        out_shape=[
            jax.ShapeDtypeStruct((steps, seqs, width), BF16),
            jax.ShapeDtypeStruct((steps, seqs, columns), BF16),
        ],
        out_specs=[pl.BlockSpec(memory_space=pltpu.HBM)] * 2,
        scratch_shapes=[
            pltpu.VMEM((steps, seqs, width), BF16),
            pltpu.VMEM((steps, seqs, columns), BF16),
            pltpu.SemaphoreType.DMA((heads * steps,)),
            pltpu.SemaphoreType.DMA((steps,)),
        ],
        compiler_params=params(16),
        cost_estimate=cost(
            4 * steps * seqs * width * steps * LANES,
            8 * steps * seqs * width + 8 * steps * seqs * columns,
            steps * seqs * width * 2,
        ),
        name="finish",
    )(back, queries, mixed, lse, *summands, *[deltas[k] for k in turns])


def body(
    hidden,
    queries,
    projection,
    cached_key_rows,
    cached_value_rows,
    adapter_shrink_weight,
    adapter_expand_weight,
    requests,
    adapter_store_row,
    lengths,
):
    steps, seqs, features = hidden.shape
    groups = lax.axis_size("dp")
    size = lax.axis_size("tp")
    cap = seqs // 4
    entries = adapter_shrink_weight.shape[0]
    heads = cached_key_rows.shape[1]

    order = [0] + sorted(range(1, groups), reverse=True)
    turns = [0, groups - 1] + list(range(1, groups - 1))
    *blocks, back = route(requests, adapter_store_row, hidden, order, cap, entries)
    over_dp = [swap("dp", groups, k) for k in order[1:]]
    over_tp = [swap("tp", size, k) for k in reversed(range(1, size))]
    got = [move(block) for move, block in zip(over_dp, blocks[1:])]

    late_hidden, _ = lax.optimization_barrier((hidden, back))
    terms = base(late_hidden.reshape(steps * seqs, features), projection, size)
    distance = size // 2
    move = swap("tp", size, distance)
    terms = [[terms[k], move(terms[distance + k])] for k in range(distance)]

    mixed, lse = past(lengths, queries, cached_key_rows, cached_value_rows)

    block, _ = lax.optimization_barrier((blocks[0], lse))
    shrunk, slots = shrink(adapter_shrink_weight, [block] + got, steps, cap)
    partial = [shrunk] + [move(shrunk) for move in over_tp]
    deltas = expand(adapter_expand_weight, partial, slots, groups)
    returned = [deltas[0]] + [move(delta) for move, delta in zip(over_dp, deltas[1:])]
    terms, _ = lax.optimization_barrier((terms, deltas[0]))
    while distance > 1:
        distance //= 2
        move = swap("tp", size, distance)
        for k in range(distance):
            moved = sum(term.astype(F32) for term in terms[distance + k]).astype(BF16)
            terms[k] = terms[k] + [move(moved)]
    summands = terms[0]
    return tuple(finish(back, summands, queries, mixed, lse, returned, turns, cap, heads))


def solution(mesh):
    placed = (
        P(None, ("rep", "dp"), "tp"),
        P(None, ("rep", "dp"), "tp"),
        P("tp", None),
        P(("rep", "dp"), "tp", None, None),
        P(("rep", "dp"), "tp", None, None),
        P("dp", None, "tp"),
        P("dp", None, "tp"),
        P(("rep", "dp")),
        P("rep"),
        P(("rep", "dp")),
    )
    return jax.shard_map(
        body,
        mesh=mesh,
        in_specs=placed,
        out_specs=(P(None, ("rep", "dp"), "tp"), P(None, ("rep", "dp"), "tp")),
        check_vma=False,
    )
```

```python
import functools
import math

import jax
import jax.numpy as jnp
from jax import lax
from jax.experimental import pallas as pl
from jax.experimental.pallas import tpu as pltpu
from jax.sharding import PartitionSpec as P

adapter_scale = 0.5
F32 = jnp.float32
BF16 = jnp.bfloat16
NT = (((1,), (1,)), ((), ()))
TN = (((0,), (0,)), ((), ()))
MIB = 1024 * 1024
LANES = 128
BASE_MIB = 53


def params(mib):
    return pltpu.CompilerParams(vmem_limit_bytes=mib * MIB)


def cost(flops, nbytes, transcendentals=0):
    return pl.CostEstimate(
        flops=int(flops), bytes_accessed=int(nbytes), transcendentals=int(transcendentals)
    )


def swap(axis, size, distance):
    pairs = [(i, i ^ distance) for i in range(size)]
    return lambda value: lax.ppermute(value, axis, pairs)


def iota(shape, dim):
    return lax.broadcasted_iota(jnp.int32, shape, dim)


def column(row):
    size = row.shape[1]
    diagonal = iota((size, size), 0) == iota((size, size), 1)
    return jnp.sum(jnp.where(diagonal, row, 0.0), axis=1, keepdims=True)


def route_kernel(order, cap, entries, requests_hbm, store_hbm, hidden_hbm, *refs):
    groups = len(order)
    blocks, back_ref = refs[:groups], refs[groups]
    requests_ref, store_ref, hidden_ref, index_sems, hidden_sems = refs[groups + 1 :]
    steps, seqs, features = hidden_ref.shape
    tiles = features // LANES
    index_copies = [
        pltpu.make_async_copy(requests_hbm, requests_ref, index_sems.at[0]),
        pltpu.make_async_copy(store_hbm, store_ref, index_sems.at[1]),
    ]
    hidden_copies = [
        pltpu.make_async_copy(hidden_hbm.at[s], hidden_ref.at[s], hidden_sems.at[s])
        for s in range(steps)
    ]
    for copy in index_copies + hidden_copies:
        copy.start()
    me = lax.axis_index("dp")
    for copy in index_copies:
        copy.wait()
    store_col = column(store_ref[...].astype(F32))
    adapters = store_col.shape[0]
    rows = jnp.sum(
        jnp.where(iota((adapters, seqs), 0) == requests_ref[...], store_col, 0.0),
        axis=0,
        keepdims=True,
    ).astype(jnp.int32)
    owner = lax.div(rows, jnp.int32(entries))
    slot_col = column((rows - owner * entries).astype(F32))
    distance = jnp.bitwise_xor(owner, me)
    turn = jnp.zeros(distance.shape, F32)
    for k, at in enumerate(order):
        turn = jnp.where(distance == at, float(k), turn)
    turn_col = column(turn)
    before = (turn_col == turn) & (iota((seqs, seqs), 0) < iota((seqs, seqs), 1))
    rank = jnp.sum(jnp.where(before, 1.0, 0.0), axis=0, keepdims=True)
    bucket = turn * cap + rank
    bucket_col = column(bucket).astype(jnp.int32)
    bucket = bucket.astype(jnp.int32)
    placed = jnp.where(iota((groups * cap, seqs), 0) == bucket, 1.0, 0.0).astype(BF16)
    back_ref[...] = jnp.where(bucket_col == iota((seqs, groups * cap), 1), 1.0, 0.0).astype(BF16)
    for k in range(groups):
        spot = lax.rem(iota((seqs, LANES), 1), jnp.int32(cap)) + k * cap
        slots = jnp.sum(jnp.where(bucket_col == spot, slot_col, 0.0), axis=0, keepdims=True)
        blocks[k][steps * tiles * cap :, :] = jnp.broadcast_to(slots, (cap, LANES)).astype(BF16)
    for s in range(steps):
        hidden_copies[s].wait()
        picked = jnp.dot(placed, hidden_ref[s], preferred_element_type=F32).astype(BF16)
        for k in range(groups):
            for c in range(tiles):
                first = (s * tiles + c) * cap
                blocks[k][first : first + cap, :] = picked[
                    k * cap : (k + 1) * cap, c * LANES : (c + 1) * LANES
                ]


def route(requests, store, hidden, order, cap, entries):
    groups = len(order)
    steps, seqs, features = hidden.shape
    rows = (steps * (features // LANES) + 1) * cap
    return pl.pallas_call(
        functools.partial(route_kernel, order, cap, entries),
        out_shape=[jax.ShapeDtypeStruct((rows, LANES), BF16)] * groups
        + [jax.ShapeDtypeStruct((seqs, groups * cap), BF16)],
        in_specs=[pl.BlockSpec(memory_space=pltpu.HBM)] * 3,
        scratch_shapes=[
            pltpu.VMEM((1, seqs), jnp.int32),
            pltpu.VMEM((1, store.shape[0]), jnp.int32),
            pltpu.VMEM(hidden.shape, BF16),
            pltpu.SemaphoreType.DMA((2,)),
            pltpu.SemaphoreType.DMA((steps,)),
        ],
        compiler_params=params(62),
        cost_estimate=cost(
            2 * groups * cap * seqs * steps * features, 4 * steps * seqs * features
        ),
        name="route",
    )(requests[None, :], store[None, :], hidden)


def base_kernel(size, hidden_hbm, projection_hbm, *refs):
    outs, (hidden_ref, projection_ref, hidden_sem, block_sems) = refs[:size], refs[size:]
    width = outs[0].shape[1]
    half = size // 2
    me = lax.axis_index("tp")
    order = list(range(half, size)) + list(range(half))
    hidden_copy = pltpu.make_async_copy(hidden_hbm, hidden_ref, hidden_sem.at[0])
    hidden_copy.start()
    copies = {}
    for k in order:
        first = pl.multiple_of(jnp.bitwise_xor(me, k) * width, width)
        copies[k] = pltpu.make_async_copy(
            projection_hbm.at[:, pl.ds(first, width)], projection_ref.at[k], block_sems.at[k]
        )
        copies[k].start()
    hidden_copy.wait()
    for k in order:
        copies[k].wait()
        part = jnp.dot(hidden_ref[...], projection_ref[k], preferred_element_type=F32)
        outs[k][...] = part.astype(outs[k].dtype)


def base(hidden, projection, size):
    rows, features = hidden.shape
    width = projection.shape[1] // size
    half = size // 2
    return pl.pallas_call(
        functools.partial(base_kernel, size),
        out_shape=[jax.ShapeDtypeStruct((rows, width), F32)] * half
        + [jax.ShapeDtypeStruct((rows, width), BF16)] * half,
        in_specs=[pl.BlockSpec(memory_space=pltpu.HBM)] * 2,
        scratch_shapes=[
            pltpu.VMEM((rows, features), BF16),
            pltpu.VMEM((size, features, width), BF16),
            pltpu.SemaphoreType.DMA((1,)),
            pltpu.SemaphoreType.DMA((size,)),
        ],
        compiler_params=params(BASE_MIB),
        cost_estimate=cost(0, 4096),
        name="base",
    )(hidden, projection)


def past_kernel(lengths_ref, query_ref, key_ref, value_ref, mixed_ref, lse_ref):
    steps, chunk, width = query_ref.shape
    _, heads, positions, size = key_ref.shape
    share = width // (size * heads)
    rows = steps * share
    first = pl.program_id(0) * chunk
    scaling = 1.0 / math.sqrt(size)

    @pl.when(first == 0)
    def _():
        lse_ref[...] = jnp.zeros_like(lse_ref)

    def lanes(g, h):
        return slice((g * share + h) * size, (g * share + h + 1) * size)

    by_seq = {}
    for s in range(steps):
        whole = query_ref[s].astype(F32)
        for g in range(heads):
            stacked = jnp.stack([whole[:, lanes(g, h)] for h in range(share)], axis=0)
            by_seq[s, g] = jnp.swapaxes(stacked, 0, 1)
    units = [(i, g) for i in range(chunk) for g in range(heads)]
    scores = []
    for i, g in units:
        q = jnp.concatenate([by_seq[s, g][i] for s in range(steps)], axis=0).astype(BF16)
        raw = lax.dot_general(q, key_ref[i, g], NT, preferred_element_type=F32) * scaling
        live = iota((rows, positions), 1) < lengths_ref[first + i]
        scores.append(jnp.where(live, raw, -jnp.inf))
    scores = jnp.concatenate(scores, axis=0)
    top = jnp.max(scores, axis=1, keepdims=True)
    raised = jnp.exp(scores - top)
    total = jnp.sum(raised, axis=1, keepdims=True)
    weights = raised.astype(BF16)
    mixed = [
        jnp.dot(weights[u * rows : (u + 1) * rows], value_ref[i, g], preferred_element_type=F32)
        for u, (i, g) in enumerate(units)
    ]
    mixed = jnp.concatenate(mixed, axis=0) * (1.0 / total)
    lse = top + jnp.log(total)
    seqs = pl.num_programs(0) * chunk
    lane = lax.rem(iota((rows, LANES), 1), seqs)
    for g in range(heads):
        packed = lse_ref[g * rows : (g + 1) * rows, :]
        for i in range(chunk):
            u = i * heads + g
            packed = jnp.where(lane == first + i, lse[u * rows : (u + 1) * rows], packed)
        lse_ref[g * rows : (g + 1) * rows, :] = packed
    mixed = mixed.reshape(chunk, heads, steps, share, size)
    for s in range(steps):
        for g in range(heads):
            mixed_by_head = jnp.swapaxes(mixed[:, g, s], 0, 1)
            for h in range(share):
                mixed_ref[s, :, lanes(g, h)] = mixed_by_head[h]


def past(lengths, queries, keys, values):
    steps, seqs, width = queries.shape
    _, heads, positions, size = keys.shape
    chunk = 8
    cache_spec = pl.BlockSpec((chunk, heads, positions, size), lambda i, n: (i, 0, 0, 0))
    return pl.pallas_call(
        past_kernel,
        grid_spec=pltpu.PrefetchScalarGridSpec(
            num_scalar_prefetch=1,
            grid=(seqs // chunk,),
            in_specs=[
                pl.BlockSpec((steps, chunk, width), lambda i, n: (0, i, 0)),
                cache_spec,
                cache_spec,
            ],
            out_specs=[
                pl.BlockSpec((steps, chunk, width), lambda i, n: (0, i, 0)),
                pl.BlockSpec((steps * width // size, LANES), lambda i, n: (0, 0)),
            ],
        ),
        out_shape=[
            jax.ShapeDtypeStruct((steps, seqs, width), F32),
            jax.ShapeDtypeStruct((steps * width // size, LANES), F32),
        ],
        compiler_params=params(16),
        cost_estimate=cost(0, 4096),
        name="past",
    )(lengths, queries, keys, values)


def slot_mask(entries, rank, slots):
    return lax.div(iota((entries * rank, slots.shape[1]), 0), jnp.int32(rank)) == slots


def shrink_kernel(count, steps, cap, entries, rank, weight_ref, *refs):
    blocks, out_ref, slot_ref = refs[:count], refs[count], refs[count + 1]
    tiles = weight_ref.shape[1] // LANES
    rows = []
    for block in blocks:
        for s in range(steps):
            places = [(s * tiles + c) * cap for c in range(tiles)]
            rows.append(jnp.concatenate([block[p : p + cap, :] for p in places], axis=1))
    rows = jnp.concatenate(rows, axis=0)
    slots = [b[steps * tiles * cap :, :][:1, : steps * cap].astype(F32) for b in blocks]
    slots = jnp.concatenate(slots, axis=1).astype(jnp.int32)
    slot_ref[...] = slots
    every = lax.dot_general(weight_ref[...], rows, NT, preferred_element_type=F32)
    kept = jnp.where(slot_mask(entries, rank, slots), every, 0.0)
    out_ref[...] = jnp.sum(kept.reshape(entries, rank, kept.shape[1]), axis=0)


def shrink(weight, blocks, steps, cap):
    entries, rank, features = weight.shape
    count = len(blocks)
    rows = count * steps * cap
    return pl.pallas_call(
        functools.partial(shrink_kernel, count, steps, cap, entries, rank),
        out_shape=[
            jax.ShapeDtypeStruct((rank, rows), F32),
            jax.ShapeDtypeStruct((1, rows), jnp.int32),
        ],
        compiler_params=params(12),
        cost_estimate=cost(
            2 * entries * rank * features * rows, 2 * features * (entries * rank + rows)
        ),
        name="shrink",
    )(weight.reshape(entries * rank, features), *blocks)


def expand_kernel(groups, size, entries, rank, weight_ref, slot_ref, *refs):
    parts, outs = refs[:size], refs[size:]
    total = parts[0][...]
    for part in parts[1:]:
        total = total + part[...]
    shrunk = total.astype(BF16).astype(F32)
    spread = jnp.broadcast_to(shrunk[None], (entries,) + shrunk.shape).reshape(
        entries * rank, shrunk.shape[1]
    )
    spread = jnp.where(slot_mask(entries, rank, slot_ref[...]), spread, 0.0).astype(BF16)
    delta = adapter_scale * lax.dot_general(
        spread, weight_ref[...], TN, preferred_element_type=F32
    )
    delta = delta.astype(BF16)
    rows = outs[0].shape[0]
    for k in range(groups):
        outs[k][...] = delta[k * rows : (k + 1) * rows]


def expand(weight, parts, slots, groups):
    entries, rank, columns = weight.shape
    rows = parts[0].shape[1] // groups
    return pl.pallas_call(
        functools.partial(expand_kernel, groups, len(parts), entries, rank),
        out_shape=[jax.ShapeDtypeStruct((rows, columns), BF16)] * groups,
        compiler_params=params(8),
        cost_estimate=cost(
            2 * entries * rank * columns * rows * groups, 2 * entries * rank * columns
        ),
        name="expand",
    )(weight.reshape(entries * rank, columns), slots, *parts)


def finish_kernel(
    turns, size, cap, heads, back_ref, query_ref, mixed_ref, lse_ref, *refs
):
    groups = len(turns)
    summands = refs[:size]
    deltas = [refs[size + turns.index(k)] for k in range(groups)]
    out_hbm, new_hbm, out_ref, new_ref, out_sems, new_sems = refs[size + groups :]
    steps, seqs, width = query_ref.shape
    columns = new_ref.shape[2]
    size = columns // (2 * heads)
    share = width // (size * heads)
    scaling = 1.0 / math.sqrt(size)
    back = back_ref[...]
    new = []
    copies = []
    for s in range(steps):
        delta = jnp.concatenate([r[s * cap : (s + 1) * cap, :] for r in deltas], axis=0)
        update = jnp.dot(back, delta, preferred_element_type=F32)
        rows = slice(s * seqs, (s + 1) * seqs)
        base = summands[0][rows, :]
        for summand in summands[1:]:
            base = base + summand[rows, :].astype(F32)
        new.append((base + update).astype(BF16))
        new_ref[s] = new[s]
        copies.append(pltpu.make_async_copy(new_ref.at[s], new_hbm.at[s], new_sems.at[s]))
        copies[-1].start()
    same = lax.rem(iota((seqs, LANES), 1), jnp.int32(seqs)) == iota((seqs, LANES), 0)

    def over_steps(parts, combine):
        whole = functools.reduce(combine, parts)
        turned = [pltpu.roll(whole, shift, 1) for shift in range(seqs, LANES, seqs)]
        return functools.reduce(combine, turned, whole)

    parts = steps * seqs // LANES
    rows = heads * steps * share
    units = [(g, s) for g in range(heads) for s in range(steps)]

    def lanes(g, h):
        return slice((g * share + h) * size, (g * share + h + 1) * size)

    fresh = [[] for _ in range(parts)]
    values = []
    for g in range(heads):
        left = g * 2 * size
        keys = jnp.concatenate([n[:, left : left + size] for n in new], axis=0)
        values.append(
            jnp.concatenate([n[:, left + size : left + 2 * size] for n in new], axis=0)
        )
        for s in range(steps):
            count = pl.cdiv((s + 1) * seqs, LANES)
            q = jnp.concatenate([query_ref[s, :, lanes(g, h)] for h in range(share)], axis=0)
            scores = lax.dot_general(q, keys[: count * LANES], NT, preferred_element_type=F32)
            for c in range(parts):
                if c < count:
                    block = scores[:, c * LANES : (c + 1) * LANES].reshape(share, seqs, LANES)
                    fresh[c].append(jnp.sum(jnp.where(same[None], block, 0.0), axis=1))
                else:
                    fresh[c].append(jnp.zeros((share, LANES), F32))
    now = lax.rem(lax.div(iota((rows, LANES), 0), jnp.int32(share)), jnp.int32(steps))
    step = lax.div(iota((rows, LANES), 1), jnp.int32(seqs))
    fresh = [
        jnp.where(
            step + c * (LANES // seqs) <= now,
            jnp.concatenate(fresh[c], axis=0) * scaling,
            -jnp.inf,
        )
        for c in range(parts)
    ]
    lse = lse_ref[...]
    top = jnp.maximum(over_steps(fresh, jnp.maximum), lse)
    old = jnp.exp(lse - top)
    raised = [jnp.exp(part - top) for part in fresh]
    scale = 1.0 / (over_steps(raised, jnp.add) + old)
    weights = [part * scale for part in raised]
    old = old * scale
    high = old.astype(BF16).astype(F32)
    halves = jnp.where(iota((rows, LANES), 1) < seqs, high, old - high)
    ones = jnp.ones((LANES, size), BF16)

    def diagonal(packed, row):
        return jnp.where(same, packed[row : row + 1], 0.0).astype(BF16)

    for g, s in units:
        count = pl.cdiv((s + 1) * seqs, LANES)
        first = (g * steps + s) * share
        spread = [
            jnp.concatenate([diagonal(part, first + h) for part in weights[:count]], axis=1)
            for h in range(share)
        ]
        mixed = jnp.dot(
            jnp.concatenate(spread, axis=0),
            values[g][: count * LANES],
            preferred_element_type=F32,
        )
        spread = [diagonal(halves, first + h) for h in range(share)]
        kept = jnp.dot(jnp.concatenate(spread, axis=0), ones, preferred_element_type=F32)
        for h in range(share):
            cut = slice(h * seqs, (h + 1) * seqs)
            total = mixed[cut] + mixed_ref[s, :, lanes(g, h)] * kept[cut]
            out_ref[s, :, lanes(g, h)] = total.astype(BF16)
        part = (s, slice(None), pl.ds(g * share * size, share * size))
        copies.append(
            pltpu.make_async_copy(
                out_ref.at[part], out_hbm.at[part], out_sems.at[g * steps + s]
            )
        )
        copies[-1].start()
    for copy in copies:
        copy.wait()


def finish(back, summands, queries, mixed, lse, deltas, turns, cap, heads):
    steps, seqs, width = queries.shape
    columns = summands[0].shape[1]
    return pl.pallas_call(
        functools.partial(finish_kernel, turns, len(summands), cap, heads),
        out_shape=[
            jax.ShapeDtypeStruct((steps, seqs, width), BF16),
            jax.ShapeDtypeStruct((steps, seqs, columns), BF16),
        ],
        out_specs=[pl.BlockSpec(memory_space=pltpu.HBM)] * 2,
        scratch_shapes=[
            pltpu.VMEM((steps, seqs, width), BF16),
            pltpu.VMEM((steps, seqs, columns), BF16),
            pltpu.SemaphoreType.DMA((heads * steps,)),
            pltpu.SemaphoreType.DMA((steps,)),
        ],
        compiler_params=params(16),
        cost_estimate=cost(
            4 * steps * seqs * width * steps * LANES,
            8 * steps * seqs * width + 8 * steps * seqs * columns,
            steps * seqs * width * 2,
        ),
        name="finish",
    )(back, queries, mixed, lse, *summands, *[deltas[k] for k in turns])


def body(
    hidden,
    queries,
    projection,
    cached_key_rows,
    cached_value_rows,
    adapter_shrink_weight,
    adapter_expand_weight,
    requests,
    adapter_store_row,
    lengths,
):
    steps, seqs, features = hidden.shape
    groups = lax.axis_size("dp")
    size = lax.axis_size("tp")
    cap = seqs // 4
    entries = adapter_shrink_weight.shape[0]
    heads = cached_key_rows.shape[1]

    order = [0] + sorted(range(1, groups), reverse=True)
    turns = [0, groups - 1] + list(range(1, groups - 1))
    *blocks, back = route(requests, adapter_store_row, hidden, order, cap, entries)
    over_dp = [swap("dp", groups, k) for k in order[1:]]
    over_tp = [swap("tp", size, k) for k in reversed(range(1, size))]
    got = [move(block) for move, block in zip(over_dp, blocks[1:])]

    late_hidden, _ = lax.optimization_barrier((hidden, back))
    terms = base(late_hidden.reshape(steps * seqs, features), projection, size)
    distance = size // 2
    move = swap("tp", size, distance)
    terms = [[terms[k], move(terms[distance + k])] for k in range(distance)]

    mixed, lse = past(lengths, queries, cached_key_rows, cached_value_rows)

    block, _ = lax.optimization_barrier((blocks[0], lse))
    shrunk, slots = shrink(adapter_shrink_weight, [block] + got, steps, cap)
    partial = [shrunk] + [move(shrunk) for move in over_tp]
    deltas = expand(adapter_expand_weight, partial, slots, groups)
    returned = [deltas[0]] + [move(delta) for move, delta in zip(over_dp, deltas[1:])]
    terms, _ = lax.optimization_barrier((terms, deltas[0]))
    while distance > 1:
        distance //= 2
        move = swap("tp", size, distance)
        for k in range(distance):
            moved = sum(term.astype(F32) for term in terms[distance + k]).astype(BF16)
            terms[k] = terms[k] + [move(moved)]
    summands = terms[0]
    return tuple(finish(back, summands, queries, mixed, lse, returned, turns, cap, heads))


def solution(mesh):
    placed = (
        P(None, ("rep", "dp"), "tp"),
        P(None, ("rep", "dp"), "tp"),
        P("tp", None),
        P(("rep", "dp"), "tp", None, None),
        P(("rep", "dp"), "tp", None, None),
        P("dp", None, "tp"),
        P("dp", None, "tp"),
        P(("rep", "dp")),
        P("rep"),
        P(("rep", "dp")),
    )
    return jax.shard_map(
        body,
        mesh=mesh,
        in_specs=placed,
        out_specs=(P(None, ("rep", "dp"), "tp"), P(None, ("rep", "dp"), "tp")),
        check_vma=False,
    )
```

```python
import functools
import math

import jax
import jax.numpy as jnp
from jax import lax
from jax.experimental import pallas as pl
from jax.experimental.pallas import tpu as pltpu
from jax.sharding import PartitionSpec as P

adapter_scale = 0.5
F32 = jnp.float32
BF16 = jnp.bfloat16
NT = (((1,), (1,)), ((), ()))
TN = (((0,), (0,)), ((), ()))
MIB = 1024 * 1024
LANES = 128
BASE_MIB = 53


def params(mib):
    return pltpu.CompilerParams(vmem_limit_bytes=mib * MIB)


def cost(flops, nbytes, transcendentals=0):
    return pl.CostEstimate(
        flops=int(flops), bytes_accessed=int(nbytes), transcendentals=int(transcendentals)
    )


def swap(axis, size, distance):
    pairs = [(i, i ^ distance) for i in range(size)]
    return lambda value: lax.ppermute(value, axis, pairs)


def iota(shape, dim):
    return lax.broadcasted_iota(jnp.int32, shape, dim)


def column(row):
    size = row.shape[1]
    diagonal = iota((size, size), 0) == iota((size, size), 1)
    return jnp.sum(jnp.where(diagonal, row, 0.0), axis=1, keepdims=True)


def route_kernel(order, cap, entries, requests_hbm, store_hbm, hidden_hbm, *refs):
    groups = len(order)
    blocks, back_ref = refs[:groups], refs[groups]
    requests_ref, store_ref, hidden_ref, index_sems, hidden_sem = refs[groups + 1 :]
    steps, seqs, features = hidden_ref.shape
    tiles = features // LANES
    index_copies = [
        pltpu.make_async_copy(requests_hbm, requests_ref, index_sems.at[0]),
        pltpu.make_async_copy(store_hbm, store_ref, index_sems.at[1]),
    ]
    hidden_copy = pltpu.make_async_copy(hidden_hbm, hidden_ref, hidden_sem.at[0])
    for copy in index_copies + [hidden_copy]:
        copy.start()
    me = lax.axis_index("dp")
    for copy in index_copies:
        copy.wait()
    store_col = column(store_ref[...].astype(F32))
    adapters = store_col.shape[0]
    rows = jnp.sum(
        jnp.where(iota((adapters, seqs), 0) == requests_ref[...], store_col, 0.0),
        axis=0,
        keepdims=True,
    ).astype(jnp.int32)
    owner = lax.div(rows, jnp.int32(entries))
    slot_col = column((rows - owner * entries).astype(F32))
    distance = jnp.bitwise_xor(owner, me)
    turn = jnp.zeros(distance.shape, F32)
    for k, at in enumerate(order):
        turn = jnp.where(distance == at, float(k), turn)
    turn_col = column(turn)
    before = (turn_col == turn) & (iota((seqs, seqs), 0) < iota((seqs, seqs), 1))
    rank = jnp.sum(jnp.where(before, 1.0, 0.0), axis=0, keepdims=True)
    bucket = turn * cap + rank
    bucket_col = column(bucket).astype(jnp.int32)
    bucket = bucket.astype(jnp.int32)
    placed = jnp.where(iota((groups * cap, seqs), 0) == bucket, 1.0, 0.0).astype(BF16)
    back_ref[...] = jnp.where(bucket_col == iota((seqs, groups * cap), 1), 1.0, 0.0).astype(BF16)
    for k in range(groups):
        spot = lax.rem(iota((seqs, LANES), 1), jnp.int32(cap)) + k * cap
        slots = jnp.sum(jnp.where(bucket_col == spot, slot_col, 0.0), axis=0, keepdims=True)
        blocks[k][steps * tiles * cap :, :] = jnp.broadcast_to(slots, (cap, LANES)).astype(BF16)
    hidden_copy.wait()
    for s in range(steps):
        picked = jnp.dot(placed, hidden_ref[s], preferred_element_type=F32).astype(BF16)
        for k in range(groups):
            for c in range(tiles):
                first = (s * tiles + c) * cap
                blocks[k][first : first + cap, :] = picked[
                    k * cap : (k + 1) * cap, c * LANES : (c + 1) * LANES
                ]


def route(requests, store, hidden, order, cap, entries):
    groups = len(order)
    steps, seqs, features = hidden.shape
    rows = (steps * (features // LANES) + 1) * cap
    return pl.pallas_call(
        functools.partial(route_kernel, order, cap, entries),
        out_shape=[jax.ShapeDtypeStruct((rows, LANES), BF16)] * groups
        + [jax.ShapeDtypeStruct((seqs, groups * cap), BF16)],
        in_specs=[pl.BlockSpec(memory_space=pltpu.HBM)] * 3,
        scratch_shapes=[
            pltpu.VMEM((1, seqs), jnp.int32),
            pltpu.VMEM((1, store.shape[0]), jnp.int32),
            pltpu.VMEM(hidden.shape, BF16),
            pltpu.SemaphoreType.DMA((2,)),
            pltpu.SemaphoreType.DMA((1,)),
        ],
        compiler_params=params(62),
        cost_estimate=cost(
            2 * groups * cap * seqs * steps * features, 4 * steps * seqs * features
        ),
        name="route",
    )(requests[None, :], store[None, :], hidden)


def base_kernel(size, hidden_hbm, projection_hbm, *refs):
    outs, (hidden_ref, projection_ref, hidden_sem, block_sems) = refs[:size], refs[size:]
    width = outs[0].shape[1]
    half = size // 2
    me = lax.axis_index("tp")
    order = list(range(half, size)) + list(range(half))
    hidden_copy = pltpu.make_async_copy(hidden_hbm, hidden_ref, hidden_sem.at[0])
    hidden_copy.start()
    copies = {}
    for k in order:
        first = pl.multiple_of(jnp.bitwise_xor(me, k) * width, width)
        copies[k] = pltpu.make_async_copy(
            projection_hbm.at[:, pl.ds(first, width)], projection_ref.at[k], block_sems.at[k]
        )
        copies[k].start()
    hidden_copy.wait()
    for k in order:
        copies[k].wait()
        part = jnp.dot(hidden_ref[...], projection_ref[k], preferred_element_type=F32)
        outs[k][...] = part.astype(outs[k].dtype)


def base(hidden, projection, size):
    rows, features = hidden.shape
    width = projection.shape[1] // size
    half = size // 2
    return pl.pallas_call(
        functools.partial(base_kernel, size),
        out_shape=[jax.ShapeDtypeStruct((rows, width), F32)] * half
        + [jax.ShapeDtypeStruct((rows, width), BF16)] * half,
        in_specs=[pl.BlockSpec(memory_space=pltpu.HBM)] * 2,
        scratch_shapes=[
            pltpu.VMEM((rows, features), BF16),
            pltpu.VMEM((size, features, width), BF16),
            pltpu.SemaphoreType.DMA((1,)),
            pltpu.SemaphoreType.DMA((size,)),
        ],
        compiler_params=params(BASE_MIB),
        cost_estimate=cost(0, 4096),
        name="base",
    )(hidden, projection)


def past_kernel(lengths_ref, query_ref, key_ref, value_ref, mixed_ref, lse_ref):
    steps, chunk, width = query_ref.shape
    _, heads, positions, size = key_ref.shape
    share = width // (size * heads)
    rows = steps * share
    first = pl.program_id(0) * chunk
    scaling = 1.0 / math.sqrt(size)

    @pl.when(first == 0)
    def _():
        lse_ref[...] = jnp.zeros_like(lse_ref)

    def lanes(g, h):
        return slice((g * share + h) * size, (g * share + h + 1) * size)

    by_seq = {}
    for s in range(steps):
        whole = query_ref[s].astype(F32)
        for g in range(heads):
            stacked = jnp.stack([whole[:, lanes(g, h)] for h in range(share)], axis=0)
            by_seq[s, g] = jnp.swapaxes(stacked, 0, 1)
    units = [(i, g) for i in range(chunk) for g in range(heads)]
    scores = []
    for i, g in units:
        q = jnp.concatenate([by_seq[s, g][i] for s in range(steps)], axis=0).astype(BF16)
        raw = lax.dot_general(q, key_ref[i, g], NT, preferred_element_type=F32) * scaling
        live = iota((rows, positions), 1) < lengths_ref[first + i]
        scores.append(jnp.where(live, raw, -jnp.inf))
    scores = jnp.concatenate(scores, axis=0)
    top = jnp.max(scores, axis=1, keepdims=True)
    raised = jnp.exp(scores - top)
    total = jnp.sum(raised, axis=1, keepdims=True)
    weights = raised.astype(BF16)
    mixed = [
        jnp.dot(weights[u * rows : (u + 1) * rows], value_ref[i, g], preferred_element_type=F32)
        for u, (i, g) in enumerate(units)
    ]
    mixed = jnp.concatenate(mixed, axis=0) * (1.0 / total)
    lse = top + jnp.log(total)
    seqs = pl.num_programs(0) * chunk
    lane = lax.rem(iota((rows, LANES), 1), seqs)
    for g in range(heads):
        packed = lse_ref[g * rows : (g + 1) * rows, :]
        for i in range(chunk):
            u = i * heads + g
            packed = jnp.where(lane == first + i, lse[u * rows : (u + 1) * rows], packed)
        lse_ref[g * rows : (g + 1) * rows, :] = packed
    mixed = mixed.reshape(chunk, heads, steps, share, size)
    for s in range(steps):
        for g in range(heads):
            mixed_by_head = jnp.swapaxes(mixed[:, g, s], 0, 1)
            for h in range(share):
                mixed_ref[s, :, lanes(g, h)] = mixed_by_head[h]


def past(lengths, queries, keys, values):
    steps, seqs, width = queries.shape
    _, heads, positions, size = keys.shape
    chunk = 8
    cache_spec = pl.BlockSpec((chunk, heads, positions, size), lambda i, n: (i, 0, 0, 0))
    return pl.pallas_call(
        past_kernel,
        grid_spec=pltpu.PrefetchScalarGridSpec(
            num_scalar_prefetch=1,
            grid=(seqs // chunk,),
            in_specs=[
                pl.BlockSpec((steps, chunk, width), lambda i, n: (0, i, 0)),
                cache_spec,
                cache_spec,
            ],
            out_specs=[
                pl.BlockSpec((steps, chunk, width), lambda i, n: (0, i, 0)),
                pl.BlockSpec((steps * width // size, LANES), lambda i, n: (0, 0)),
            ],
        ),
        out_shape=[
            jax.ShapeDtypeStruct((steps, seqs, width), F32),
            jax.ShapeDtypeStruct((steps * width // size, LANES), F32),
        ],
        compiler_params=params(16),
        cost_estimate=cost(0, 4096),
        name="past",
    )(lengths, queries, keys, values)


def slot_mask(entries, rank, slots):
    return lax.div(iota((entries * rank, slots.shape[1]), 0), jnp.int32(rank)) == slots


def shrink_kernel(count, steps, cap, entries, rank, weight_ref, *refs):
    blocks, out_ref, slot_ref = refs[:count], refs[count], refs[count + 1]
    tiles = weight_ref.shape[1] // LANES
    rows = []
    for block in blocks:
        for s in range(steps):
            places = [(s * tiles + c) * cap for c in range(tiles)]
            rows.append(jnp.concatenate([block[p : p + cap, :] for p in places], axis=1))
    rows = jnp.concatenate(rows, axis=0)
    slots = [b[steps * tiles * cap :, :][:1, : steps * cap].astype(F32) for b in blocks]
    slots = jnp.concatenate(slots, axis=1).astype(jnp.int32)
    slot_ref[...] = slots
    every = lax.dot_general(weight_ref[...], rows, NT, preferred_element_type=F32)
    kept = jnp.where(slot_mask(entries, rank, slots), every, 0.0)
    out_ref[...] = jnp.sum(kept.reshape(entries, rank, kept.shape[1]), axis=0)


def shrink(weight, blocks, steps, cap):
    entries, rank, features = weight.shape
    count = len(blocks)
    rows = count * steps * cap
    return pl.pallas_call(
        functools.partial(shrink_kernel, count, steps, cap, entries, rank),
        out_shape=[
            jax.ShapeDtypeStruct((rank, rows), F32),
            jax.ShapeDtypeStruct((1, rows), jnp.int32),
        ],
        compiler_params=params(12),
        cost_estimate=cost(
            2 * entries * rank * features * rows, 2 * features * (entries * rank + rows)
        ),
        name="shrink",
    )(weight.reshape(entries * rank, features), *blocks)


def expand_kernel(groups, size, entries, rank, weight_ref, slot_ref, *refs):
    parts, outs = refs[:size], refs[size:]
    total = parts[0][...]
    for part in parts[1:]:
        total = total + part[...]
    shrunk = total.astype(BF16).astype(F32)
    spread = jnp.broadcast_to(shrunk[None], (entries,) + shrunk.shape).reshape(
        entries * rank, shrunk.shape[1]
    )
    spread = jnp.where(slot_mask(entries, rank, slot_ref[...]), spread, 0.0).astype(BF16)
    delta = adapter_scale * lax.dot_general(
        spread, weight_ref[...], TN, preferred_element_type=F32
    )
    delta = delta.astype(BF16)
    rows = outs[0].shape[0]
    for k in range(groups):
        outs[k][...] = delta[k * rows : (k + 1) * rows]


def expand(weight, parts, slots, groups):
    entries, rank, columns = weight.shape
    rows = parts[0].shape[1] // groups
    return pl.pallas_call(
        functools.partial(expand_kernel, groups, len(parts), entries, rank),
        out_shape=[jax.ShapeDtypeStruct((rows, columns), BF16)] * groups,
        compiler_params=params(8),
        cost_estimate=cost(
            2 * entries * rank * columns * rows * groups, 2 * entries * rank * columns
        ),
        name="expand",
    )(weight.reshape(entries * rank, columns), slots, *parts)


def finish_kernel(
    turns, size, cap, heads, back_ref, query_ref, mixed_ref, lse_ref, *refs
):
    groups = len(turns)
    summands = refs[:size]
    deltas = [refs[size + turns.index(k)] for k in range(groups)]
    out_hbm, new_hbm, out_ref, new_ref, out_sems, new_sem = refs[size + groups :]
    steps, seqs, width = query_ref.shape
    columns = new_ref.shape[2]
    size = columns // (2 * heads)
    share = width // (size * heads)
    scaling = 1.0 / math.sqrt(size)
    back = back_ref[...]
    new = []
    copies = []
    for s in range(steps):
        delta = jnp.concatenate([r[s * cap : (s + 1) * cap, :] for r in deltas], axis=0)
        update = jnp.dot(back, delta, preferred_element_type=F32)
        rows = slice(s * seqs, (s + 1) * seqs)
        base = summands[0][rows, :]
        for summand in summands[1:]:
            base = base + summand[rows, :].astype(F32)
        new.append((base + update).astype(BF16))
        new_ref[s] = new[s]
    copies.append(pltpu.make_async_copy(new_ref, new_hbm, new_sem.at[0]))
    copies[-1].start()
    same = lax.rem(iota((seqs, LANES), 1), jnp.int32(seqs)) == iota((seqs, LANES), 0)

    def over_steps(parts, combine):
        whole = functools.reduce(combine, parts)
        turned = [pltpu.roll(whole, shift, 1) for shift in range(seqs, LANES, seqs)]
        return functools.reduce(combine, turned, whole)

    parts = steps * seqs // LANES
    rows = heads * steps * share
    units = [(g, s) for g in range(heads) for s in range(steps)]

    def lanes(g, h):
        return slice((g * share + h) * size, (g * share + h + 1) * size)

    fresh = [[] for _ in range(parts)]
    values = []
    for g in range(heads):
        left = g * 2 * size
        keys = jnp.concatenate([n[:, left : left + size] for n in new], axis=0)
        values.append(
            jnp.concatenate([n[:, left + size : left + 2 * size] for n in new], axis=0)
        )
        for s in range(steps):
            count = pl.cdiv((s + 1) * seqs, LANES)
            q = jnp.concatenate([query_ref[s, :, lanes(g, h)] for h in range(share)], axis=0)
            scores = lax.dot_general(q, keys[: count * LANES], NT, preferred_element_type=F32)
            for c in range(parts):
                if c < count:
                    block = scores[:, c * LANES : (c + 1) * LANES].reshape(share, seqs, LANES)
                    fresh[c].append(jnp.sum(jnp.where(same[None], block, 0.0), axis=1))
                else:
                    fresh[c].append(jnp.zeros((share, LANES), F32))
    now = lax.rem(lax.div(iota((rows, LANES), 0), jnp.int32(share)), jnp.int32(steps))
    step = lax.div(iota((rows, LANES), 1), jnp.int32(seqs))
    fresh = [
        jnp.where(
            step + c * (LANES // seqs) <= now,
            jnp.concatenate(fresh[c], axis=0) * scaling,
            -jnp.inf,
        )
        for c in range(parts)
    ]
    lse = lse_ref[...]
    top = jnp.maximum(over_steps(fresh, jnp.maximum), lse)
    old = jnp.exp(lse - top)
    raised = [jnp.exp(part - top) for part in fresh]
    scale = 1.0 / (over_steps(raised, jnp.add) + old)
    weights = [part * scale for part in raised]
    old = old * scale
    high = old.astype(BF16).astype(F32)
    halves = jnp.where(iota((rows, LANES), 1) < seqs, high, old - high)
    ones = jnp.ones((LANES, size), BF16)

    def diagonal(packed, row):
        return jnp.where(same, packed[row : row + 1], 0.0).astype(BF16)

    for g, s in units:
        count = pl.cdiv((s + 1) * seqs, LANES)
        first = (g * steps + s) * share
        spread = [
            jnp.concatenate([diagonal(part, first + h) for part in weights[:count]], axis=1)
            for h in range(share)
        ]
        mixed = jnp.dot(
            jnp.concatenate(spread, axis=0),
            values[g][: count * LANES],
            preferred_element_type=F32,
        )
        spread = [diagonal(halves, first + h) for h in range(share)]
        kept = jnp.dot(jnp.concatenate(spread, axis=0), ones, preferred_element_type=F32)
        for h in range(share):
            cut = slice(h * seqs, (h + 1) * seqs)
            total = mixed[cut] + mixed_ref[s, :, lanes(g, h)] * kept[cut]
            out_ref[s, :, lanes(g, h)] = total.astype(BF16)
        part = (s, slice(None), pl.ds(g * share * size, share * size))
        copies.append(
            pltpu.make_async_copy(
                out_ref.at[part], out_hbm.at[part], out_sems.at[g * steps + s]
            )
        )
        copies[-1].start()
    for copy in copies:
        copy.wait()


def finish(back, summands, queries, mixed, lse, deltas, turns, cap, heads):
    steps, seqs, width = queries.shape
    columns = summands[0].shape[1]
    return pl.pallas_call(
        functools.partial(finish_kernel, turns, len(summands), cap, heads),
        out_shape=[
            jax.ShapeDtypeStruct((steps, seqs, width), BF16),
            jax.ShapeDtypeStruct((steps, seqs, columns), BF16),
        ],
        out_specs=[pl.BlockSpec(memory_space=pltpu.HBM)] * 2,
        scratch_shapes=[
            pltpu.VMEM((steps, seqs, width), BF16),
            pltpu.VMEM((steps, seqs, columns), BF16),
            pltpu.SemaphoreType.DMA((heads * steps,)),
            pltpu.SemaphoreType.DMA((1,)),
        ],
        compiler_params=params(16),
        cost_estimate=cost(
            4 * steps * seqs * width * steps * LANES,
            8 * steps * seqs * width + 8 * steps * seqs * columns,
            steps * seqs * width * 2,
        ),
        name="finish",
    )(back, queries, mixed, lse, *summands, *[deltas[k] for k in turns])


def body(
    hidden,
    queries,
    projection,
    cached_key_rows,
    cached_value_rows,
    adapter_shrink_weight,
    adapter_expand_weight,
    requests,
    adapter_store_row,
    lengths,
):
    steps, seqs, features = hidden.shape
    groups = lax.axis_size("dp")
    size = lax.axis_size("tp")
    cap = seqs // 4
    entries = adapter_shrink_weight.shape[0]
    heads = cached_key_rows.shape[1]

    order = [0] + sorted(range(1, groups), reverse=True)
    turns = [0, groups - 1] + list(range(1, groups - 1))
    *blocks, back = route(requests, adapter_store_row, hidden, order, cap, entries)
    over_dp = [swap("dp", groups, k) for k in order[1:]]
    over_tp = [swap("tp", size, k) for k in reversed(range(1, size))]
    got = [move(block) for move, block in zip(over_dp, blocks[1:])]

    late_hidden, _ = lax.optimization_barrier((hidden, back))
    terms = base(late_hidden.reshape(steps * seqs, features), projection, size)
    distance = size // 2
    move = swap("tp", size, distance)
    terms = [[terms[k], move(terms[distance + k])] for k in range(distance)]

    mixed, lse = past(lengths, queries, cached_key_rows, cached_value_rows)

    block, _ = lax.optimization_barrier((blocks[0], lse))
    shrunk, slots = shrink(adapter_shrink_weight, [block] + got, steps, cap)
    partial = [shrunk] + [move(shrunk) for move in over_tp]
    deltas = expand(adapter_expand_weight, partial, slots, groups)
    returned = [deltas[0]] + [move(delta) for move, delta in zip(over_dp, deltas[1:])]
    terms, _ = lax.optimization_barrier((terms, deltas[0]))
    while distance > 1:
        distance //= 2
        move = swap("tp", size, distance)
        for k in range(distance):
            moved = sum(term.astype(F32) for term in terms[distance + k]).astype(BF16)
            terms[k] = terms[k] + [move(moved)]
    summands = terms[0]
    return tuple(finish(back, summands, queries, mixed, lse, returned, turns, cap, heads))


def solution(mesh):
    placed = (
        P(None, ("rep", "dp"), "tp"),
        P(None, ("rep", "dp"), "tp"),
        P("tp", None),
        P(("rep", "dp"), "tp", None, None),
        P(("rep", "dp"), "tp", None, None),
        P("dp", None, "tp"),
        P("dp", None, "tp"),
        P(("rep", "dp")),
        P("rep"),
        P(("rep", "dp")),
    )
    return jax.shard_map(
        body,
        mesh=mesh,
        in_specs=placed,
        out_specs=(P(None, ("rep", "dp"), "tp"), P(None, ("rep", "dp"), "tp")),
        check_vma=False,
    )
```

```python
import functools
import math

import jax
import jax.numpy as jnp
from jax import lax
from jax.experimental import pallas as pl
from jax.experimental.pallas import tpu as pltpu
from jax.sharding import PartitionSpec as P

adapter_scale = 0.5
F32 = jnp.float32
BF16 = jnp.bfloat16
NT = (((1,), (1,)), ((), ()))
TN = (((0,), (0,)), ((), ()))
MIB = 1024 * 1024
LANES = 128
BASE_MIB = 53


def params(mib):
    return pltpu.CompilerParams(vmem_limit_bytes=mib * MIB)


def cost(flops, nbytes, transcendentals=0):
    return pl.CostEstimate(
        flops=int(flops), bytes_accessed=int(nbytes), transcendentals=int(transcendentals)
    )


def swap(axis, size, distance):
    pairs = [(i, i ^ distance) for i in range(size)]
    return lambda value: lax.ppermute(value, axis, pairs)


def iota(shape, dim):
    return lax.broadcasted_iota(jnp.int32, shape, dim)


def column(row):
    size = row.shape[1]
    diagonal = iota((size, size), 0) == iota((size, size), 1)
    return jnp.sum(jnp.where(diagonal, row, 0.0), axis=1, keepdims=True)


def route_kernel(order, cap, entries, requests_hbm, store_hbm, hidden_hbm, *refs):
    groups = len(order)
    blocks, back_ref = refs[:groups], refs[groups]
    requests_ref, store_ref, hidden_ref, index_sems, hidden_sem = refs[groups + 1 :]
    steps, seqs, features = hidden_ref.shape
    tiles = features // LANES
    index_copies = [
        pltpu.make_async_copy(requests_hbm, requests_ref, index_sems.at[0]),
        pltpu.make_async_copy(store_hbm, store_ref, index_sems.at[1]),
    ]
    hidden_copy = pltpu.make_async_copy(hidden_hbm, hidden_ref, hidden_sem.at[0])
    for copy in index_copies + [hidden_copy]:
        copy.start()
    me = lax.axis_index("dp")
    for copy in index_copies:
        copy.wait()
    store_col = column(store_ref[...].astype(F32))
    adapters = store_col.shape[0]
    rows = jnp.sum(
        jnp.where(iota((adapters, seqs), 0) == requests_ref[...], store_col, 0.0),
        axis=0,
        keepdims=True,
    ).astype(jnp.int32)
    owner = lax.div(rows, jnp.int32(entries))
    slot_col = column((rows - owner * entries).astype(F32))
    distance = jnp.bitwise_xor(owner, me)
    turn = jnp.zeros(distance.shape, F32)
    for k, at in enumerate(order):
        turn = jnp.where(distance == at, float(k), turn)
    turn_col = column(turn)
    before = (turn_col == turn) & (iota((seqs, seqs), 0) < iota((seqs, seqs), 1))
    rank = jnp.sum(jnp.where(before, 1.0, 0.0), axis=0, keepdims=True)
    bucket = turn * cap + rank
    bucket_col = column(bucket).astype(jnp.int32)
    bucket = bucket.astype(jnp.int32)
    placed = jnp.where(iota((groups * cap, seqs), 0) == bucket, 1.0, 0.0).astype(BF16)
    back_ref[...] = jnp.where(bucket_col == iota((seqs, groups * cap), 1), 1.0, 0.0).astype(BF16)
    for k in range(groups):
        spot = lax.rem(iota((seqs, LANES), 1), jnp.int32(cap)) + k * cap
        slots = jnp.sum(jnp.where(bucket_col == spot, slot_col, 0.0), axis=0, keepdims=True)
        blocks[k][steps * tiles * cap :, :] = jnp.broadcast_to(slots, (cap, LANES)).astype(BF16)
    hidden_copy.wait()
    for s in range(steps):
        picked = jnp.dot(placed, hidden_ref[s], preferred_element_type=F32).astype(BF16)
        for k in range(groups):
            for c in range(tiles):
                first = (s * tiles + c) * cap
                blocks[k][first : first + cap, :] = picked[
                    k * cap : (k + 1) * cap, c * LANES : (c + 1) * LANES
                ]


def route(requests, store, hidden, order, cap, entries):
    groups = len(order)
    steps, seqs, features = hidden.shape
    rows = (steps * (features // LANES) + 1) * cap
    return pl.pallas_call(
        functools.partial(route_kernel, order, cap, entries),
        out_shape=[jax.ShapeDtypeStruct((rows, LANES), BF16)] * groups
        + [jax.ShapeDtypeStruct((seqs, groups * cap), BF16)],
        in_specs=[pl.BlockSpec(memory_space=pltpu.HBM)] * 3,
        scratch_shapes=[
            pltpu.VMEM((1, seqs), jnp.int32),
            pltpu.VMEM((1, store.shape[0]), jnp.int32),
            pltpu.VMEM(hidden.shape, BF16),
            pltpu.SemaphoreType.DMA((2,)),
            pltpu.SemaphoreType.DMA((1,)),
        ],
        compiler_params=params(62),
        cost_estimate=cost(
            2 * groups * cap * seqs * steps * features, 4 * steps * seqs * features
        ),
        name="route",
    )(requests[None, :], store[None, :], hidden)


def base_kernel(size, hidden_hbm, projection_hbm, *refs):
    outs, (hidden_ref, projection_ref, hidden_sem, block_sems) = refs[:size], refs[size:]
    width = outs[0].shape[1]
    half = size // 2
    me = lax.axis_index("tp")
    order = list(range(half, size)) + list(range(half))
    hidden_copy = pltpu.make_async_copy(hidden_hbm, hidden_ref, hidden_sem.at[0])
    hidden_copy.start()
    copies = {}
    for k in order:
        first = pl.multiple_of(jnp.bitwise_xor(me, k) * width, width)
        copies[k] = pltpu.make_async_copy(
            projection_hbm.at[:, pl.ds(first, width)], projection_ref.at[k], block_sems.at[k]
        )
        copies[k].start()
    hidden_copy.wait()
    for k in order:
        copies[k].wait()
        part = jnp.dot(hidden_ref[...], projection_ref[k], preferred_element_type=F32)
        outs[k][...] = part.astype(outs[k].dtype)


def base(hidden, projection, size):
    rows, features = hidden.shape
    width = projection.shape[1] // size
    half = size // 2
    return pl.pallas_call(
        functools.partial(base_kernel, size),
        out_shape=[jax.ShapeDtypeStruct((rows, width), F32)] * half
        + [jax.ShapeDtypeStruct((rows, width), BF16)] * half,
        in_specs=[pl.BlockSpec(memory_space=pltpu.HBM)] * 2,
        scratch_shapes=[
            pltpu.VMEM((rows, features), BF16),
            pltpu.VMEM((size, features, width), BF16),
            pltpu.SemaphoreType.DMA((1,)),
            pltpu.SemaphoreType.DMA((size,)),
        ],
        compiler_params=params(BASE_MIB),
        cost_estimate=cost(0, 4096),
        name="base",
    )(hidden, projection)


def past_kernel(lengths_ref, query_ref, key_ref, value_ref, mixed_ref, lse_ref):
    steps, chunk, width = query_ref.shape
    _, heads, positions, size = key_ref.shape
    share = width // (size * heads)
    rows = steps * share
    first = pl.program_id(0) * chunk
    scaling = 1.0 / math.sqrt(size)

    @pl.when(first == 0)
    def _():
        lse_ref[...] = jnp.zeros_like(lse_ref)

    def lanes(g, h):
        return slice((g * share + h) * size, (g * share + h + 1) * size)

    by_seq = {}
    for s in range(steps):
        whole = query_ref[s].astype(F32)
        for g in range(heads):
            stacked = jnp.stack([whole[:, lanes(g, h)] for h in range(share)], axis=0)
            by_seq[s, g] = jnp.swapaxes(stacked, 0, 1)
    units = [(i, g) for i in range(chunk) for g in range(heads)]
    scores = []
    for i, g in units:
        q = jnp.concatenate([by_seq[s, g][i] for s in range(steps)], axis=0).astype(BF16)
        raw = lax.dot_general(q, key_ref[i, g], NT, preferred_element_type=F32) * scaling
        live = iota((rows, positions), 1) < lengths_ref[first + i]
        scores.append(jnp.where(live, raw, -jnp.inf))
    scores = jnp.concatenate(scores, axis=0)
    top = jnp.max(scores, axis=1, keepdims=True)
    raised = jnp.exp(scores - top)
    total = jnp.sum(raised, axis=1, keepdims=True)
    weights = raised.astype(BF16)
    mixed = [
        jnp.dot(weights[u * rows : (u + 1) * rows], value_ref[i, g], preferred_element_type=F32)
        for u, (i, g) in enumerate(units)
    ]
    mixed = jnp.concatenate(mixed, axis=0) * (1.0 / total)
    lse = top + jnp.log(total)
    seqs = pl.num_programs(0) * chunk
    lane = lax.rem(iota((rows, LANES), 1), seqs)
    for g in range(heads):
        packed = lse_ref[g * rows : (g + 1) * rows, :]
        for i in range(chunk):
            u = i * heads + g
            packed = jnp.where(lane == first + i, lse[u * rows : (u + 1) * rows], packed)
        lse_ref[g * rows : (g + 1) * rows, :] = packed
    mixed = mixed.reshape(chunk, heads, steps, share, size)
    for s in range(steps):
        for g in range(heads):
            mixed_by_head = jnp.swapaxes(mixed[:, g, s], 0, 1)
            for h in range(share):
                mixed_ref[s, :, lanes(g, h)] = mixed_by_head[h]


def past(lengths, queries, keys, values):
    steps, seqs, width = queries.shape
    _, heads, positions, size = keys.shape
    chunk = 16
    cache_spec = pl.BlockSpec((chunk, heads, positions, size), lambda i, n: (i, 0, 0, 0))
    return pl.pallas_call(
        past_kernel,
        grid_spec=pltpu.PrefetchScalarGridSpec(
            num_scalar_prefetch=1,
            grid=(seqs // chunk,),
            in_specs=[
                pl.BlockSpec((steps, chunk, width), lambda i, n: (0, i, 0)),
                cache_spec,
                cache_spec,
            ],
            out_specs=[
                pl.BlockSpec((steps, chunk, width), lambda i, n: (0, i, 0)),
                pl.BlockSpec((steps * width // size, LANES), lambda i, n: (0, 0)),
            ],
        ),
        out_shape=[
            jax.ShapeDtypeStruct((steps, seqs, width), F32),
            jax.ShapeDtypeStruct((steps * width // size, LANES), F32),
        ],
        compiler_params=params(16),
        cost_estimate=cost(0, 4096),
        name="past",
    )(lengths, queries, keys, values)


def slot_mask(entries, rank, slots):
    return lax.div(iota((entries * rank, slots.shape[1]), 0), jnp.int32(rank)) == slots


def shrink_kernel(count, steps, cap, entries, rank, weight_ref, *refs):
    blocks, out_ref, slot_ref = refs[:count], refs[count], refs[count + 1]
    tiles = weight_ref.shape[1] // LANES
    rows = []
    for block in blocks:
        for s in range(steps):
            places = [(s * tiles + c) * cap for c in range(tiles)]
            rows.append(jnp.concatenate([block[p : p + cap, :] for p in places], axis=1))
    rows = jnp.concatenate(rows, axis=0)
    slots = [b[steps * tiles * cap :, :][:1, : steps * cap].astype(F32) for b in blocks]
    slots = jnp.concatenate(slots, axis=1).astype(jnp.int32)
    slot_ref[...] = slots
    every = lax.dot_general(weight_ref[...], rows, NT, preferred_element_type=F32)
    kept = jnp.where(slot_mask(entries, rank, slots), every, 0.0)
    out_ref[...] = jnp.sum(kept.reshape(entries, rank, kept.shape[1]), axis=0)


def shrink(weight, blocks, steps, cap):
    entries, rank, features = weight.shape
    count = len(blocks)
    rows = count * steps * cap
    return pl.pallas_call(
        functools.partial(shrink_kernel, count, steps, cap, entries, rank),
        out_shape=[
            jax.ShapeDtypeStruct((rank, rows), F32),
            jax.ShapeDtypeStruct((1, rows), jnp.int32),
        ],
        compiler_params=params(12),
        cost_estimate=cost(
            2 * entries * rank * features * rows, 2 * features * (entries * rank + rows)
        ),
        name="shrink",
    )(weight.reshape(entries * rank, features), *blocks)


def expand_kernel(groups, size, entries, rank, weight_ref, slot_ref, *refs):
    parts, outs = refs[:size], refs[size:]
    total = parts[0][...]
    for part in parts[1:]:
        total = total + part[...]
    shrunk = total.astype(BF16).astype(F32)
    spread = jnp.broadcast_to(shrunk[None], (entries,) + shrunk.shape).reshape(
        entries * rank, shrunk.shape[1]
    )
    spread = jnp.where(slot_mask(entries, rank, slot_ref[...]), spread, 0.0).astype(BF16)
    delta = adapter_scale * lax.dot_general(
        spread, weight_ref[...], TN, preferred_element_type=F32
    )
    delta = delta.astype(BF16)
    rows = outs[0].shape[0]
    for k in range(groups):
        outs[k][...] = delta[k * rows : (k + 1) * rows]


def expand(weight, parts, slots, groups):
    entries, rank, columns = weight.shape
    rows = parts[0].shape[1] // groups
    return pl.pallas_call(
        functools.partial(expand_kernel, groups, len(parts), entries, rank),
        out_shape=[jax.ShapeDtypeStruct((rows, columns), BF16)] * groups,
        compiler_params=params(8),
        cost_estimate=cost(
            2 * entries * rank * columns * rows * groups, 2 * entries * rank * columns
        ),
        name="expand",
    )(weight.reshape(entries * rank, columns), slots, *parts)


def finish_kernel(
    turns, size, cap, heads, back_ref, query_ref, mixed_ref, lse_ref, *refs
):
    groups = len(turns)
    summands = refs[:size]
    deltas = [refs[size + turns.index(k)] for k in range(groups)]
    out_hbm, new_hbm, out_ref, new_ref, out_sems, new_sem = refs[size + groups :]
    steps, seqs, width = query_ref.shape
    columns = new_ref.shape[2]
    size = columns // (2 * heads)
    share = width // (size * heads)
    scaling = 1.0 / math.sqrt(size)
    back = back_ref[...]
    new = []
    copies = []
    for s in range(steps):
        delta = jnp.concatenate([r[s * cap : (s + 1) * cap, :] for r in deltas], axis=0)
        update = jnp.dot(back, delta, preferred_element_type=F32)
        rows = slice(s * seqs, (s + 1) * seqs)
        base = summands[0][rows, :]
        for summand in summands[1:]:
            base = base + summand[rows, :].astype(F32)
        new.append((base + update).astype(BF16))
        new_ref[s] = new[s]
    copies.append(pltpu.make_async_copy(new_ref, new_hbm, new_sem.at[0]))
    copies[-1].start()
    same = lax.rem(iota((seqs, LANES), 1), jnp.int32(seqs)) == iota((seqs, LANES), 0)

    def over_steps(parts, combine):
        whole = functools.reduce(combine, parts)
        turned = [pltpu.roll(whole, shift, 1) for shift in range(seqs, LANES, seqs)]
        return functools.reduce(combine, turned, whole)

    parts = steps * seqs // LANES
    rows = heads * steps * share
    units = [(g, s) for g in range(heads) for s in range(steps)]

    def lanes(g, h):
        return slice((g * share + h) * size, (g * share + h + 1) * size)

    fresh = [[] for _ in range(parts)]
    values = []
    for g in range(heads):
        left = g * 2 * size
        keys = jnp.concatenate([n[:, left : left + size] for n in new], axis=0)
        values.append(
            jnp.concatenate([n[:, left + size : left + 2 * size] for n in new], axis=0)
        )
        for s in range(steps):
            count = pl.cdiv((s + 1) * seqs, LANES)
            q = jnp.concatenate([query_ref[s, :, lanes(g, h)] for h in range(share)], axis=0)
            scores = lax.dot_general(q, keys[: count * LANES], NT, preferred_element_type=F32)
            for c in range(parts):
                if c < count:
                    block = scores[:, c * LANES : (c + 1) * LANES].reshape(share, seqs, LANES)
                    fresh[c].append(jnp.sum(jnp.where(same[None], block, 0.0), axis=1))
                else:
                    fresh[c].append(jnp.zeros((share, LANES), F32))
    now = lax.rem(lax.div(iota((rows, LANES), 0), jnp.int32(share)), jnp.int32(steps))
    step = lax.div(iota((rows, LANES), 1), jnp.int32(seqs))
    fresh = [
        jnp.where(
            step + c * (LANES // seqs) <= now,
            jnp.concatenate(fresh[c], axis=0) * scaling,
            -jnp.inf,
        )
        for c in range(parts)
    ]
    lse = lse_ref[...]
    top = jnp.maximum(over_steps(fresh, jnp.maximum), lse)
    old = jnp.exp(lse - top)
    raised = [jnp.exp(part - top) for part in fresh]
    scale = 1.0 / (over_steps(raised, jnp.add) + old)
    weights = [part * scale for part in raised]
    old = old * scale
    high = old.astype(BF16).astype(F32)
    halves = jnp.where(iota((rows, LANES), 1) < seqs, high, old - high)
    ones = jnp.ones((LANES, size), BF16)

    def diagonal(packed, row):
        return jnp.where(same, packed[row : row + 1], 0.0).astype(BF16)

    for g, s in units:
        count = pl.cdiv((s + 1) * seqs, LANES)
        first = (g * steps + s) * share
        spread = [
            jnp.concatenate([diagonal(part, first + h) for part in weights[:count]], axis=1)
            for h in range(share)
        ]
        mixed = jnp.dot(
            jnp.concatenate(spread, axis=0),
            values[g][: count * LANES],
            preferred_element_type=F32,
        )
        spread = [diagonal(halves, first + h) for h in range(share)]
        kept = jnp.dot(jnp.concatenate(spread, axis=0), ones, preferred_element_type=F32)
        for h in range(share):
            cut = slice(h * seqs, (h + 1) * seqs)
            total = mixed[cut] + mixed_ref[s, :, lanes(g, h)] * kept[cut]
            out_ref[s, :, lanes(g, h)] = total.astype(BF16)
        part = (s, slice(None), pl.ds(g * share * size, share * size))
        copies.append(
            pltpu.make_async_copy(
                out_ref.at[part], out_hbm.at[part], out_sems.at[g * steps + s]
            )
        )
        copies[-1].start()
    for copy in copies:
        copy.wait()


def finish(back, summands, queries, mixed, lse, deltas, turns, cap, heads):
    steps, seqs, width = queries.shape
    columns = summands[0].shape[1]
    return pl.pallas_call(
        functools.partial(finish_kernel, turns, len(summands), cap, heads),
        out_shape=[
            jax.ShapeDtypeStruct((steps, seqs, width), BF16),
            jax.ShapeDtypeStruct((steps, seqs, columns), BF16),
        ],
        out_specs=[pl.BlockSpec(memory_space=pltpu.HBM)] * 2,
        scratch_shapes=[
            pltpu.VMEM((steps, seqs, width), BF16),
            pltpu.VMEM((steps, seqs, columns), BF16),
            pltpu.SemaphoreType.DMA((heads * steps,)),
            pltpu.SemaphoreType.DMA((1,)),
        ],
        compiler_params=params(16),
        cost_estimate=cost(
            4 * steps * seqs * width * steps * LANES,
            8 * steps * seqs * width + 8 * steps * seqs * columns,
            steps * seqs * width * 2,
        ),
        name="finish",
    )(back, queries, mixed, lse, *summands, *[deltas[k] for k in turns])


def body(
    hidden,
    queries,
    projection,
    cached_key_rows,
    cached_value_rows,
    adapter_shrink_weight,
    adapter_expand_weight,
    requests,
    adapter_store_row,
    lengths,
):
    steps, seqs, features = hidden.shape
    groups = lax.axis_size("dp")
    size = lax.axis_size("tp")
    cap = seqs // 4
    entries = adapter_shrink_weight.shape[0]
    heads = cached_key_rows.shape[1]

    order = [0] + sorted(range(1, groups), reverse=True)
    turns = [0, groups - 1] + list(range(1, groups - 1))
    *blocks, back = route(requests, adapter_store_row, hidden, order, cap, entries)
    over_dp = [swap("dp", groups, k) for k in order[1:]]
    over_tp = [swap("tp", size, k) for k in reversed(range(1, size))]
    got = [move(block) for move, block in zip(over_dp, blocks[1:])]

    late_hidden, _ = lax.optimization_barrier((hidden, back))
    terms = base(late_hidden.reshape(steps * seqs, features), projection, size)
    distance = size // 2
    move = swap("tp", size, distance)
    terms = [[terms[k], move(terms[distance + k])] for k in range(distance)]

    mixed, lse = past(lengths, queries, cached_key_rows, cached_value_rows)

    block, _ = lax.optimization_barrier((blocks[0], lse))
    shrunk, slots = shrink(adapter_shrink_weight, [block] + got, steps, cap)
    partial = [shrunk] + [move(shrunk) for move in over_tp]
    deltas = expand(adapter_expand_weight, partial, slots, groups)
    returned = [deltas[0]] + [move(delta) for move, delta in zip(over_dp, deltas[1:])]
    terms, _ = lax.optimization_barrier((terms, deltas[0]))
    while distance > 1:
        distance //= 2
        move = swap("tp", size, distance)
        for k in range(distance):
            moved = sum(term.astype(F32) for term in terms[distance + k]).astype(BF16)
            terms[k] = terms[k] + [move(moved)]
    summands = terms[0]
    return tuple(finish(back, summands, queries, mixed, lse, returned, turns, cap, heads))


def solution(mesh):
    placed = (
        P(None, ("rep", "dp"), "tp"),
        P(None, ("rep", "dp"), "tp"),
        P("tp", None),
        P(("rep", "dp"), "tp", None, None),
        P(("rep", "dp"), "tp", None, None),
        P("dp", None, "tp"),
        P("dp", None, "tp"),
        P(("rep", "dp")),
        P("rep"),
        P(("rep", "dp")),
    )
    return jax.shard_map(
        body,
        mesh=mesh,
        in_specs=placed,
        out_specs=(P(None, ("rep", "dp"), "tp"), P(None, ("rep", "dp"), "tp")),
        check_vma=False,
    )
```

```python
import functools
import math

import jax
import jax.numpy as jnp
from jax import lax
from jax.experimental import pallas as pl
from jax.experimental.pallas import tpu as pltpu
from jax.sharding import PartitionSpec as P

adapter_scale = 0.5
F32 = jnp.float32
BF16 = jnp.bfloat16
NT = (((1,), (1,)), ((), ()))
TN = (((0,), (0,)), ((), ()))
MIB = 1024 * 1024
LANES = 128
BASE_MIB = 53


def params(mib):
    return pltpu.CompilerParams(vmem_limit_bytes=mib * MIB)


def cost(flops, nbytes, transcendentals=0):
    return pl.CostEstimate(
        flops=int(flops), bytes_accessed=int(nbytes), transcendentals=int(transcendentals)
    )


def swap(axis, size, distance):
    pairs = [(i, i ^ distance) for i in range(size)]
    return lambda value: lax.ppermute(value, axis, pairs)


def iota(shape, dim):
    return lax.broadcasted_iota(jnp.int32, shape, dim)


def column(row):
    size = row.shape[1]
    diagonal = iota((size, size), 0) == iota((size, size), 1)
    return jnp.sum(jnp.where(diagonal, row, 0.0), axis=1, keepdims=True)


def route_kernel(order, cap, entries, requests_hbm, store_hbm, hidden_hbm, *refs):
    groups = len(order)
    blocks, back_ref = refs[:groups], refs[groups]
    requests_ref, store_ref, hidden_ref, index_sems, hidden_sem = refs[groups + 1 :]
    steps, seqs, features = hidden_ref.shape
    tiles = features // LANES
    index_copies = [
        pltpu.make_async_copy(requests_hbm, requests_ref, index_sems.at[0]),
        pltpu.make_async_copy(store_hbm, store_ref, index_sems.at[1]),
    ]
    hidden_copy = pltpu.make_async_copy(hidden_hbm, hidden_ref, hidden_sem.at[0])
    for copy in index_copies + [hidden_copy]:
        copy.start()
    me = lax.axis_index("dp")
    for copy in index_copies:
        copy.wait()
    store_col = column(store_ref[...].astype(F32))
    adapters = store_col.shape[0]
    rows = jnp.sum(
        jnp.where(iota((adapters, seqs), 0) == requests_ref[...], store_col, 0.0),
        axis=0,
        keepdims=True,
    ).astype(jnp.int32)
    owner = lax.div(rows, jnp.int32(entries))
    slot_col = column((rows - owner * entries).astype(F32))
    distance = jnp.bitwise_xor(owner, me)
    turn = jnp.zeros(distance.shape, F32)
    for k, at in enumerate(order):
        turn = jnp.where(distance == at, float(k), turn)
    turn_col = column(turn)
    before = (turn_col == turn) & (iota((seqs, seqs), 0) < iota((seqs, seqs), 1))
    rank = jnp.sum(jnp.where(before, 1.0, 0.0), axis=0, keepdims=True)
    bucket = turn * cap + rank
    bucket_col = column(bucket).astype(jnp.int32)
    bucket = bucket.astype(jnp.int32)
    placed = jnp.where(iota((groups * cap, seqs), 0) == bucket, 1.0, 0.0).astype(BF16)
    back_ref[...] = jnp.where(bucket_col == iota((seqs, groups * cap), 1), 1.0, 0.0).astype(BF16)
    for k in range(groups):
        spot = lax.rem(iota((seqs, LANES), 1), jnp.int32(cap)) + k * cap
        slots = jnp.sum(jnp.where(bucket_col == spot, slot_col, 0.0), axis=0, keepdims=True)
        blocks[k][steps * tiles * cap :, :] = jnp.broadcast_to(slots, (cap, LANES)).astype(BF16)
    hidden_copy.wait()
    for s in range(steps):
        picked = jnp.dot(placed, hidden_ref[s], preferred_element_type=F32).astype(BF16)
        for k in range(groups):
            for c in range(tiles):
                first = (s * tiles + c) * cap
                blocks[k][first : first + cap, :] = picked[
                    k * cap : (k + 1) * cap, c * LANES : (c + 1) * LANES
                ]


def route(requests, store, hidden, order, cap, entries):
    groups = len(order)
    steps, seqs, features = hidden.shape
    rows = (steps * (features // LANES) + 1) * cap
    return pl.pallas_call(
        functools.partial(route_kernel, order, cap, entries),
        out_shape=[jax.ShapeDtypeStruct((rows, LANES), BF16)] * groups
        + [jax.ShapeDtypeStruct((seqs, groups * cap), BF16)],
        in_specs=[pl.BlockSpec(memory_space=pltpu.HBM)] * 3,
        scratch_shapes=[
            pltpu.VMEM((1, seqs), jnp.int32),
            pltpu.VMEM((1, store.shape[0]), jnp.int32),
            pltpu.VMEM(hidden.shape, BF16),
            pltpu.SemaphoreType.DMA((2,)),
            pltpu.SemaphoreType.DMA((1,)),
        ],
        compiler_params=params(62),
        cost_estimate=cost(
            2 * groups * cap * seqs * steps * features, 4 * steps * seqs * features
        ),
        name="route",
    )(requests[None, :], store[None, :], hidden)


def base_kernel(size, hidden_hbm, projection_hbm, *refs):
    outs, (hidden_ref, projection_ref, hidden_sem, block_sems) = refs[:size], refs[size:]
    width = outs[0].shape[1]
    half = size // 2
    me = lax.axis_index("tp")
    order = list(range(half, size)) + list(range(half))
    hidden_copy = pltpu.make_async_copy(hidden_hbm, hidden_ref, hidden_sem.at[0])
    hidden_copy.start()
    copies = {}
    for k in order:
        first = pl.multiple_of(jnp.bitwise_xor(me, k) * width, width)
        copies[k] = pltpu.make_async_copy(
            projection_hbm.at[:, pl.ds(first, width)], projection_ref.at[k], block_sems.at[k]
        )
        copies[k].start()
    hidden_copy.wait()
    for k in order:
        copies[k].wait()
        part = jnp.dot(hidden_ref[...], projection_ref[k], preferred_element_type=F32)
        outs[k][...] = part.astype(outs[k].dtype)


def base(hidden, projection, size):
    rows, features = hidden.shape
    width = projection.shape[1] // size
    half = size // 2
    return pl.pallas_call(
        functools.partial(base_kernel, size),
        out_shape=[jax.ShapeDtypeStruct((rows, width), F32)] * half
        + [jax.ShapeDtypeStruct((rows, width), BF16)] * half,
        in_specs=[pl.BlockSpec(memory_space=pltpu.HBM)] * 2,
        scratch_shapes=[
            pltpu.VMEM((rows, features), BF16),
            pltpu.VMEM((size, features, width), BF16),
            pltpu.SemaphoreType.DMA((1,)),
            pltpu.SemaphoreType.DMA((size,)),
        ],
        compiler_params=params(BASE_MIB),
        cost_estimate=cost(0, 4096),
        name="base",
    )(hidden, projection)


def past_kernel(lengths_ref, query_ref, key_ref, value_ref, mixed_ref, lse_ref):
    steps, chunk, width = query_ref.shape
    _, heads, positions, size = key_ref.shape
    share = width // (size * heads)
    rows = steps * share
    first = pl.program_id(0) * chunk
    scaling = 1.0 / math.sqrt(size)

    @pl.when(first == 0)
    def _():
        lse_ref[...] = jnp.zeros_like(lse_ref)

    def lanes(g, h):
        return slice((g * share + h) * size, (g * share + h + 1) * size)

    by_seq = {}
    for s in range(steps):
        whole = query_ref[s].astype(F32)
        for g in range(heads):
            stacked = jnp.stack([whole[:, lanes(g, h)] for h in range(share)], axis=0)
            by_seq[s, g] = jnp.swapaxes(stacked, 0, 1)
    units = [(i, g) for i in range(chunk) for g in range(heads)]
    scores = []
    for i, g in units:
        q = jnp.concatenate([by_seq[s, g][i] for s in range(steps)], axis=0).astype(BF16)
        raw = lax.dot_general(q, key_ref[i, g], NT, preferred_element_type=F32) * scaling
        live = iota((rows, positions), 1) < lengths_ref[first + i]
        scores.append(jnp.where(live, raw, -jnp.inf))
    scores = jnp.concatenate(scores, axis=0)
    top = jnp.max(scores, axis=1, keepdims=True)
    raised = jnp.exp(scores - top)
    total = jnp.sum(raised, axis=1, keepdims=True)
    weights = raised.astype(BF16)
    mixed = [
        jnp.dot(weights[u * rows : (u + 1) * rows], value_ref[i, g], preferred_element_type=F32)
        for u, (i, g) in enumerate(units)
    ]
    mixed = jnp.concatenate(mixed, axis=0) * (1.0 / total)
    lse = top + jnp.log(total)
    seqs = pl.num_programs(0) * chunk
    lane = lax.rem(iota((rows, LANES), 1), seqs)
    for g in range(heads):
        packed = lse_ref[g * rows : (g + 1) * rows, :]
        for i in range(chunk):
            u = i * heads + g
            packed = jnp.where(lane == first + i, lse[u * rows : (u + 1) * rows], packed)
        lse_ref[g * rows : (g + 1) * rows, :] = packed
    mixed = mixed.reshape(chunk, heads, steps, share, size)
    for s in range(steps):
        for g in range(heads):
            mixed_by_head = jnp.swapaxes(mixed[:, g, s], 0, 1)
            for h in range(share):
                mixed_ref[s, :, lanes(g, h)] = mixed_by_head[h]


def past(lengths, queries, keys, values):
    steps, seqs, width = queries.shape
    _, heads, positions, size = keys.shape
    chunk = 16
    cache_spec = pl.BlockSpec((chunk, heads, positions, size), lambda i, n: (i, 0, 0, 0))
    return pl.pallas_call(
        past_kernel,
        grid_spec=pltpu.PrefetchScalarGridSpec(
            num_scalar_prefetch=1,
            grid=(seqs // chunk,),
            in_specs=[
                pl.BlockSpec((steps, chunk, width), lambda i, n: (0, i, 0)),
                cache_spec,
                cache_spec,
            ],
            out_specs=[
                pl.BlockSpec((steps, chunk, width), lambda i, n: (0, i, 0)),
                pl.BlockSpec((steps * width // size, LANES), lambda i, n: (0, 0)),
            ],
        ),
        out_shape=[
            jax.ShapeDtypeStruct((steps, seqs, width), F32),
            jax.ShapeDtypeStruct((steps * width // size, LANES), F32),
        ],
        compiler_params=params(16),
        cost_estimate=cost(0, 4096),
        name="past",
    )(lengths, queries, keys, values)


def slot_mask(entries, rank, slots):
    return lax.div(iota((entries * rank, slots.shape[1]), 0), jnp.int32(rank)) == slots


def shrink_kernel(count, steps, cap, entries, rank, weight_ref, *refs):
    blocks, early, (out_ref, slot_ref) = refs[:count], refs[count:-2], refs[-2:]
    before = early[0].shape[1] if early else 0
    if early:
        out_ref[:, :before] = early[0][...]
        slot_ref[:, :before] = early[1][...]
    tiles = weight_ref.shape[1] // LANES
    rows = []
    for block in blocks:
        for s in range(steps):
            places = [(s * tiles + c) * cap for c in range(tiles)]
            rows.append(jnp.concatenate([block[p : p + cap, :] for p in places], axis=1))
    rows = jnp.concatenate(rows, axis=0)
    slots = [b[steps * tiles * cap :, :][:1, : steps * cap].astype(F32) for b in blocks]
    slots = jnp.concatenate(slots, axis=1).astype(jnp.int32)
    slot_ref[:, before:] = slots
    every = lax.dot_general(weight_ref[...], rows, NT, preferred_element_type=F32)
    kept = jnp.where(slot_mask(entries, rank, slots), every, 0.0)
    out_ref[:, before:] = jnp.sum(kept.reshape(entries, rank, kept.shape[1]), axis=0)


def shrink(weight, blocks, steps, cap, early=()):
    entries, rank, features = weight.shape
    count = len(blocks)
    rows = count * steps * cap + (early[0].shape[1] if early else 0)
    return pl.pallas_call(
        functools.partial(shrink_kernel, count, steps, cap, entries, rank),
        out_shape=[
            jax.ShapeDtypeStruct((rank, rows), F32),
            jax.ShapeDtypeStruct((1, rows), jnp.int32),
        ],
        compiler_params=params(12),
        cost_estimate=cost(
            2 * entries * rank * features * rows, 2 * features * (entries * rank + rows)
        ),
        name="shrink",
    )(weight.reshape(entries * rank, features), *blocks, *early)


def expand_kernel(groups, size, entries, rank, weight_ref, slot_ref, *refs):
    parts, outs = refs[:size], refs[size:]
    total = parts[0][...]
    for part in parts[1:]:
        total = total + part[...]
    shrunk = total.astype(BF16).astype(F32)
    spread = jnp.broadcast_to(shrunk[None], (entries,) + shrunk.shape).reshape(
        entries * rank, shrunk.shape[1]
    )
    spread = jnp.where(slot_mask(entries, rank, slot_ref[...]), spread, 0.0).astype(BF16)
    delta = adapter_scale * lax.dot_general(
        spread, weight_ref[...], TN, preferred_element_type=F32
    )
    delta = delta.astype(BF16)
    rows = outs[0].shape[0]
    for k in range(groups):
        outs[k][...] = delta[k * rows : (k + 1) * rows]


def expand(weight, parts, slots, groups):
    entries, rank, columns = weight.shape
    rows = parts[0].shape[1] // groups
    return pl.pallas_call(
        functools.partial(expand_kernel, groups, len(parts), entries, rank),
        out_shape=[jax.ShapeDtypeStruct((rows, columns), BF16)] * groups,
        compiler_params=params(8),
        cost_estimate=cost(
            2 * entries * rank * columns * rows * groups, 2 * entries * rank * columns
        ),
        name="expand",
    )(weight.reshape(entries * rank, columns), slots, *parts)


def finish_kernel(
    turns, size, cap, heads, back_ref, query_ref, mixed_ref, lse_ref, *refs
):
    groups = len(turns)
    summands = refs[:size]
    deltas = [refs[size + turns.index(k)] for k in range(groups)]
    out_hbm, new_hbm, out_ref, new_ref, out_sems, new_sem = refs[size + groups :]
    steps, seqs, width = query_ref.shape
    columns = new_ref.shape[2]
    size = columns // (2 * heads)
    share = width // (size * heads)
    scaling = 1.0 / math.sqrt(size)
    back = back_ref[...]
    new = []
    copies = []
    for s in range(steps):
        delta = jnp.concatenate([r[s * cap : (s + 1) * cap, :] for r in deltas], axis=0)
        update = jnp.dot(back, delta, preferred_element_type=F32)
        rows = slice(s * seqs, (s + 1) * seqs)
        base = summands[0][rows, :]
        for summand in summands[1:]:
            base = base + summand[rows, :].astype(F32)
        new.append((base + update).astype(BF16))
        new_ref[s] = new[s]
    copies.append(pltpu.make_async_copy(new_ref, new_hbm, new_sem.at[0]))
    copies[-1].start()
    same = lax.rem(iota((seqs, LANES), 1), jnp.int32(seqs)) == iota((seqs, LANES), 0)

    def over_steps(parts, combine):
        whole = functools.reduce(combine, parts)
        turned = [pltpu.roll(whole, shift, 1) for shift in range(seqs, LANES, seqs)]
        return functools.reduce(combine, turned, whole)

    parts = steps * seqs // LANES
    rows = heads * steps * share
    units = [(g, s) for g in range(heads) for s in range(steps)]

    def lanes(g, h):
        return slice((g * share + h) * size, (g * share + h + 1) * size)

    fresh = [[] for _ in range(parts)]
    values = []
    for g in range(heads):
        left = g * 2 * size
        keys = jnp.concatenate([n[:, left : left + size] for n in new], axis=0)
        values.append(
            jnp.concatenate([n[:, left + size : left + 2 * size] for n in new], axis=0)
        )
        for s in range(steps):
            count = pl.cdiv((s + 1) * seqs, LANES)
            q = jnp.concatenate([query_ref[s, :, lanes(g, h)] for h in range(share)], axis=0)
            scores = lax.dot_general(q, keys[: count * LANES], NT, preferred_element_type=F32)
            for c in range(parts):
                if c < count:
                    block = scores[:, c * LANES : (c + 1) * LANES].reshape(share, seqs, LANES)
                    fresh[c].append(jnp.sum(jnp.where(same[None], block, 0.0), axis=1))
                else:
                    fresh[c].append(jnp.zeros((share, LANES), F32))
    now = lax.rem(lax.div(iota((rows, LANES), 0), jnp.int32(share)), jnp.int32(steps))
    step = lax.div(iota((rows, LANES), 1), jnp.int32(seqs))
    fresh = [
        jnp.where(
            step + c * (LANES // seqs) <= now,
            jnp.concatenate(fresh[c], axis=0) * scaling,
            -jnp.inf,
        )
        for c in range(parts)
    ]
    lse = lse_ref[...]
    top = jnp.maximum(over_steps(fresh, jnp.maximum), lse)
    old = jnp.exp(lse - top)
    raised = [jnp.exp(part - top) for part in fresh]
    scale = 1.0 / (over_steps(raised, jnp.add) + old)
    weights = [part * scale for part in raised]
    old = old * scale
    high = old.astype(BF16).astype(F32)
    halves = jnp.where(iota((rows, LANES), 1) < seqs, high, old - high)
    ones = jnp.ones((LANES, size), BF16)

    def diagonal(packed, row):
        return jnp.where(same, packed[row : row + 1], 0.0).astype(BF16)

    for g, s in units:
        count = pl.cdiv((s + 1) * seqs, LANES)
        first = (g * steps + s) * share
        spread = [
            jnp.concatenate([diagonal(part, first + h) for part in weights[:count]], axis=1)
            for h in range(share)
        ]
        mixed = jnp.dot(
            jnp.concatenate(spread, axis=0),
            values[g][: count * LANES],
            preferred_element_type=F32,
        )
        spread = [diagonal(halves, first + h) for h in range(share)]
        kept = jnp.dot(jnp.concatenate(spread, axis=0), ones, preferred_element_type=F32)
        for h in range(share):
            cut = slice(h * seqs, (h + 1) * seqs)
            total = mixed[cut] + mixed_ref[s, :, lanes(g, h)] * kept[cut]
            out_ref[s, :, lanes(g, h)] = total.astype(BF16)
        part = (s, slice(None), pl.ds(g * share * size, share * size))
        copies.append(
            pltpu.make_async_copy(
                out_ref.at[part], out_hbm.at[part], out_sems.at[g * steps + s]
            )
        )
        copies[-1].start()
    for copy in copies:
        copy.wait()


def finish(back, summands, queries, mixed, lse, deltas, turns, cap, heads):
    steps, seqs, width = queries.shape
    columns = summands[0].shape[1]
    return pl.pallas_call(
        functools.partial(finish_kernel, turns, len(summands), cap, heads),
        out_shape=[
            jax.ShapeDtypeStruct((steps, seqs, width), BF16),
            jax.ShapeDtypeStruct((steps, seqs, columns), BF16),
        ],
        out_specs=[pl.BlockSpec(memory_space=pltpu.HBM)] * 2,
        scratch_shapes=[
            pltpu.VMEM((steps, seqs, width), BF16),
            pltpu.VMEM((steps, seqs, columns), BF16),
            pltpu.SemaphoreType.DMA((heads * steps,)),
            pltpu.SemaphoreType.DMA((1,)),
        ],
        compiler_params=params(16),
        cost_estimate=cost(
            4 * steps * seqs * width * steps * LANES,
            8 * steps * seqs * width + 8 * steps * seqs * columns,
            steps * seqs * width * 2,
        ),
        name="finish",
    )(back, queries, mixed, lse, *summands, *[deltas[k] for k in turns])


def body(
    hidden,
    queries,
    projection,
    cached_key_rows,
    cached_value_rows,
    adapter_shrink_weight,
    adapter_expand_weight,
    requests,
    adapter_store_row,
    lengths,
):
    steps, seqs, features = hidden.shape
    groups = lax.axis_size("dp")
    size = lax.axis_size("tp")
    cap = seqs // 4
    entries = adapter_shrink_weight.shape[0]
    heads = cached_key_rows.shape[1]

    order = [0] + sorted(range(1, groups), reverse=True)
    turns = [0] + list(reversed(range(1, groups)))
    *blocks, back = route(requests, adapter_store_row, hidden, order, cap, entries)
    over_dp = [swap("dp", groups, k) for k in order[1:]]
    over_tp = [swap("tp", size, k) for k in reversed(range(1, size))]
    got = [move(block) for move, block in zip(over_dp, blocks[1:])]

    late_hidden, _ = lax.optimization_barrier((hidden, back))
    terms = base(late_hidden.reshape(steps * seqs, features), projection, size)
    distance = size // 2
    move = swap("tp", size, distance)
    terms = [[terms[k], move(terms[distance + k])] for k in range(distance)]

    mixed, lse = past(lengths, queries, cached_key_rows, cached_value_rows)

    block, _ = lax.optimization_barrier((blocks[0], lse))
    half = groups // 2
    early = shrink(adapter_shrink_weight, [block] + got[: half - 1], steps, cap)
    shrunk, slots = shrink(adapter_shrink_weight, got[half - 1 :], steps, cap, early)
    partial = [shrunk] + [move(shrunk) for move in over_tp]
    deltas = expand(adapter_expand_weight, partial, slots, groups)
    returned = [deltas[0]] + [move(delta) for move, delta in zip(over_dp, deltas[1:])]
    terms, _ = lax.optimization_barrier((terms, deltas[0]))
    while distance > 1:
        distance //= 2
        move = swap("tp", size, distance)
        for k in range(distance):
            moved = sum(term.astype(F32) for term in terms[distance + k]).astype(BF16)
            terms[k] = terms[k] + [move(moved)]
    summands = terms[0]
    return tuple(finish(back, summands, queries, mixed, lse, returned, turns, cap, heads))


def solution(mesh):
    placed = (
        P(None, ("rep", "dp"), "tp"),
        P(None, ("rep", "dp"), "tp"),
        P("tp", None),
        P(("rep", "dp"), "tp", None, None),
        P(("rep", "dp"), "tp", None, None),
        P("dp", None, "tp"),
        P("dp", None, "tp"),
        P(("rep", "dp")),
        P("rep"),
        P(("rep", "dp")),
    )
    return jax.shard_map(
        body,
        mesh=mesh,
        in_specs=placed,
        out_specs=(P(None, ("rep", "dp"), "tp"), P(None, ("rep", "dp"), "tp")),
        check_vma=False,
    )
```
